32 devices in a mesh: yaw: 4 (over y, x), space: 8 (over z, core).
Axes of the slice: x: 2, y: 2, z: 4, core: 2. Of those that a mesh axis runs over, the one named last changes fastest.
Arguments:
- adjoint: float32 [4, 4, 16, 32, 256], P('yaw', None, 'space'), may hold values from -6 to 6
- viscosity: float32 [4, 16, 32, 256], P('yaw', 'space'), may hold values from 0.25 to 4
- coupling: float32 [4, 4, 4], P('yaw'), may hold values from -3 to 3
- yaw_weight: float32 [4], P('yaw'), may hold values from 0.03 to 0.3
- node_cell: int32 [16384], P('space'), may hold values from 0 to 16383
- node_patch: int32 [16384], P('space'), may hold values from 0 to 2047
- node_normal: float32 [3, 16384], P(None, 'space'), may hold values from -5 to 5
- morph_kernel: float32 [2048, 256], P('space'), may hold values from -0.375 to 0.375
Outputs:
- residual: float32 [4, 4, 16, 32, 256], P('yaw', None, 'space')
- patch_gradient: float32 [3, 2048], P(None, 'space')
- node_gradient: float32 [3, 16384], P(None, 'space')
The draws below stay inside these ranges and needn't reach their ends.
Inputs may be any that keep to these rules, and one draw needn't show every extreme that they name: node_cell[n] indexes a cell of slab n // 2048, flattened over its 2 x 32 x 256 cells in that order.
All inputs are finite; a program needn't handle non-finite values.
Results may differ from the reference program's by a relative error of at most 0.000098.
Values sent between devices are 32-bit elements; how exact they have to be, the bound alone decides.
A program may use at most 64 MiB of HBM per device.

```python
import math
import jax
import jax.numpy as jnp
from jax import lax

FIELDS = 4
CX = 2
NY = 32
NZ = 256
NODES_DEV = 2048
PN_DEV = 256
YAW = 4
NX = 16
NODES = 16384
PNODES = 2048
N_SPACE = 8


def touch_ends(values, own_key, least, top_value):
    shape = values.shape
    spot = [jax.random.randint(jax.random.fold_in(own_key, axis), (), 0, shape[axis]) for axis in range(len(shape))]
    values = values.at[tuple(spot)].set(least)
    longest = shape.index(max(shape))
    spot[longest] = (spot[longest] + 1) % shape[longest]
    return values.at[tuple(spot)].set(top_value)


def block_scale(key, shape, pieces, least, largest):
    def one(position, parts):
        steps = jax.random.uniform(jax.random.fold_in(jax.random.fold_in(key, 6), position), (parts,), jnp.float32, least / len(pieces), largest / len(pieces))
        return jnp.repeat(jnp.exp(steps), shape[position] // parts).reshape((-1,) + (1,) * (len(shape) - position - 1))

    factor_of = one(*pieces[0])
    for cut in pieces[1:]:
        factor_of = factor_of * one(*cut)
    return factor_of


def normal_values(own_key, shape, width, limit, pieces=(), dtype=jnp.bfloat16):
    drawn = width * jax.random.normal(own_key, shape, jnp.float32)
    if pieces:
        drawn = drawn * block_scale(own_key, shape, pieces, -0.22, 0.18)
    return jnp.clip(drawn, -limit, limit).astype(dtype)


def setup_inputs(seed: int = 0) -> dict:
    splits = jax.random.split(jax.random.key(seed), 9)
    adjoint = normal_values(splits[0], (YAW, FIELDS, NX, NY, NZ), 1.0, 6.0, ((0, 4), (2, 8)), jnp.float32)
    viscosity = jnp.clip(jnp.exp(math.log(4.0) - 2.7725887 * jax.random.uniform(splits[1], (YAW, NX, NY, NZ), jnp.float32) ** block_scale(splits[1], (YAW, NX, NY, NZ), ((0, 4), (1, 8)), -0.2, 0.2)), 0.25, 4.0)
    coupling = normal_values(splits[2], (YAW, FIELDS, FIELDS), 0.5, 3.0, ((0, 4),), jnp.float32)
    yaw_weight = jnp.clip(jnp.exp(math.log(0.3) - 2.3025852 * jax.random.uniform(splits[3], (YAW,), jnp.float32) ** block_scale(splits[3], (YAW,), ((0, 4),), -0.2, 0.2)), 0.03, 0.3)
    node_cell = touch_ends(jax.random.randint(splits[4], (NODES,), 0, CX * NY * NZ), jax.random.fold_in(splits[4], 1), 0, (CX * NY * NZ) - 1).astype(jnp.int32)
    node_patch = touch_ends(jax.random.randint(splits[5], (NODES,), 0, PNODES), jax.random.fold_in(splits[5], 1), 0, PNODES - 1).astype(jnp.int32)
    node_normal = normal_values(splits[6], (3, NODES), 1.0, 5.0, ((1, 8),), jnp.float32)
    morph_kernel = normal_values(splits[7], (PNODES, PN_DEV), PN_DEV ** -0.5, 0.375, ((0, 8),), jnp.float32)
    return dict(adjoint=adjoint, viscosity=viscosity, coupling=coupling, yaw_weight=yaw_weight, node_cell=node_cell, node_patch=node_patch, node_normal=node_normal, morph_kernel=morph_kernel)


def window(array, starts):
    for index, start in enumerate(starts):
        axis = array.ndim - 3 + index
        array = lax.slice_in_dim(array, start, start + array.shape[axis] - 2, axis=axis)
    return array


def face_flux(grid):
    fields = grid[..., :-1, :, :, :]
    visc = grid[..., -1:, :, :, :]
    centre_f = window(fields, (1, 1, 1))
    centre_v = window(visc, (1, 1, 1))
    flux = jnp.zeros_like(centre_f)
    for starts in ((0, 1, 1), (2, 1, 1), (1, 0, 1), (1, 2, 1), (1, 1, 0), (1, 1, 2)):
        flux = flux + 0.5 * (centre_v + window(visc, starts)) * (window(fields, starts) - centre_f)
    return flux


def member_residual(member):
    adj, visc, coup = member
    grid = jnp.concatenate([adj, visc[None]], axis=0)
    grid = jnp.pad(grid, ((0, 0), (1, 1), (1, 1), (1, 1)))
    flux = face_flux(grid)
    coupled = jnp.dot(coup, adj.reshape(adj.shape[0], -1), precision=lax.Precision.HIGHEST).reshape(adj.shape)
    return coupled + 2.0 * adj - flux


def reference(adjoint, viscosity, coupling, yaw_weight, node_cell, node_patch, node_normal, morph_kernel):
    residual = lax.map(member_residual, (adjoint, viscosity, coupling))
    slab = (jnp.arange(NODES) // NODES_DEV).astype(jnp.int32)
    adj_flat = adjoint.reshape(YAW, FIELDS, N_SPACE, CX * NY * NZ)
    res_flat = residual.reshape(YAW, FIELDS, N_SPACE, CX * NY * NZ)
    visc_flat = viscosity.reshape(YAW, N_SPACE, CX * NY * NZ)
    adj_at = adj_flat[:, :, slab, node_cell]
    res_at = res_flat[:, :, slab, node_cell]
    visc_at = visc_flat[:, slab, node_cell]
    sens = visc_at * jnp.sum(adj_at * res_at, axis=1)
    weighted = jnp.sum(yaw_weight[:, None] * sens, axis=0)
    node_part = node_normal * weighted[None, :]
    patch_sum = jax.ops.segment_sum(node_part.T, node_patch, num_segments=PNODES).T
    blocks = patch_sum.reshape(3, N_SPACE, PN_DEV)
    kernel = morph_kernel.reshape(N_SPACE, PN_DEV, PN_DEV)
    smoothed = blocks + jnp.einsum("spq,csq->csp", kernel, blocks, precision=lax.Precision.HIGHEST)
    patch_gradient = smoothed.reshape(3, PNODES)
    node_gradient = patch_gradient[:, node_patch]
    return residual, patch_gradient, node_gradient
```

```python
import functools

import jax
import jax.numpy as jnp
from jax import lax
from jax.experimental import pallas as pl
from jax.experimental.pallas import tpu as pltpu
from jax.sharding import PartitionSpec as P

LANES = 128
CHUNK = 256
F32 = jnp.float32
BF16 = jnp.bfloat16


def dot(a, b, contract=((1,), (0,))):
    return lax.dot_general(a, b, (contract, ((), ())), preferred_element_type=F32)


def parts(x):
    hi = x.astype(BF16)
    return hi, (x - hi.astype(F32)).astype(BF16)


def each(count, body, first=1):
    if count <= 8:
        for d in range(first, count):
            body(d)
    else:
        lax.fori_loop(first, count, lambda d, c: (body(d), c)[1], 0)


def kernel(
    n_yaw, n_space,
    coup_in, weight_in, adj_in, visc_in, cell_in, patch_in, normal_in, morph_in,
    res, pgrad, grads_out, patch, pick_patch,
    coup, weight, adj, visc, cell, normal, morph,
    before_a, before_v, after_a, after_v,
    pick_row, pick_patch_t, normal8, morph_hi, morph_lo,
    dense, got, grads,
    row_in, load, halo_send, halo_recv, send1, recv1, send3, recv3, morph_send, morph_recv,
):
    _, fields, layers, ny, nz = adj.shape
    nodes = cell.shape[1]
    owned = morph.shape[1]
    halves = owned // LANES
    used = 3 * halves
    rows = dense.shape[1]
    groups = nz // LANES
    y0, s0 = lax.axis_index("yaw"), lax.axis_index("space")

    def space_peer(d):
        return lax.rem(s0 + d, n_space)

    def yaw_peer(d):
        return lax.rem(y0 + d, n_yaw)

    has_before, has_after = s0 > 0, s0 < n_space - 1

    def enter(d):
        pl.semaphore_signal(barrier, inc=1, device_id={"space": space_peer(d)})

    barrier = pltpu.get_barrier_semaphore()
    enter(n_space - 1)
    if n_space > 2:
        enter(1)
    loads = [
        pltpu.make_async_copy(src, dst, load.at[i])
        for i, (src, dst) in enumerate((
            (adj_in, adj), (visc_in, visc), (coup_in, coup), (cell_in, cell), (patch_in, patch),
            (normal_in, normal), (weight_in, weight),
        ))
    ]
    for copy in loads[:2]:
        copy.start()
    each(n_space - 1, enter, 2)
    each(n_yaw, lambda d: pl.semaphore_signal(barrier, inc=1, device_id={"yaw": yaw_peer(d)}))
    for copy in loads[2:]:
        copy.start()
    grads[...] = jnp.zeros_like(grads)

    core = lax.rem(s0, 2)
    first = s0 - core
    turn = lax.rem(y0, 2)
    mine = first + turn
    is_site = core == 1
    own_morph = pltpu.make_async_copy(morph_in, morph, load.at[7])
    near_morph = pltpu.make_async_remote_copy(
        src_ref=morph_in, dst_ref=morph, send_sem=morph_send, recv_sem=morph_recv,
        device_id={"space": first + 1},
    )
    uses_own = jnp.logical_and(is_site, turn == 1)
    gets_near = jnp.logical_and(is_site, turn == 0)
    gives_near = jnp.logical_and(core == 0, turn == 0)

    @pl.when(uses_own)
    def _():
        own_morph.start()

    pl.semaphore_wait(barrier, n_space + n_yaw - 2)

    def halo(slot, src, dst, peer):
        return pltpu.make_async_remote_copy(
            src_ref=src, dst_ref=dst, send_sem=halo_send.at[slot], recv_sem=halo_recv.at[slot],
            device_id={"space": peer},
        )

    up = (
        halo(0, adj.at[0, :, layers - 1], before_a, s0 + 1),
        halo(1, visc.at[0, layers - 1], before_v, s0 + 1),
    )
    down = (
        halo(2, adj_in.at[0, :, 0], after_a, s0 - 1),
        halo(3, visc_in.at[0, 0], after_v, s0 - 1),
    )

    @pl.when(has_before)
    def _():
        for copy in down:
            copy.start()

    for copy in loads[:2]:
        copy.wait()

    @pl.when(has_after)
    def _():
        for copy in up:
            copy.start()

    each(n_yaw, lambda d: pl.semaphore_signal(row_in, inc=1, device_id={"yaw": yaw_peer(d)}))

    @pl.when(gives_near)
    def _():
        near_morph.start()

    @pl.when(jnp.logical_not(has_before))
    def _():
        before_a[...] = jnp.zeros_like(before_a)
        before_v[...] = jnp.zeros_like(before_v)

    @pl.when(jnp.logical_not(has_after))
    def _():
        after_a[...] = jnp.zeros_like(after_a)
        after_v[...] = jnp.zeros_like(after_v)

    for copy in loads[2:]:
        copy.wait()

    at_y = lax.broadcasted_iota(jnp.int32, (ny, nz), 0)
    at_z = lax.broadcasted_iota(jnp.int32, (ny, nz), 1)
    shifts = (
        (0, 1, at_y > 0), (0, ny - 1, at_y < ny - 1), (1, 1, at_z > 0), (1, nz - 1, at_z < nz - 1)
    )
    for x in range(layers):
        v = visc[0, x]
        total = jnp.zeros_like(v)
        faces = []
        for axis, shift, inside in shifts:
            face = 0.5 * (v + jnp.where(inside, pltpu.roll(v, shift, axis), 0.0))
            total = total + face
            faces.append(jnp.where(inside, face, 0.0))
        inner = {}
        for nb in (x - 1, x + 1):
            if 0 <= nb < layers:
                inner[nb] = 0.5 * (v + visc[0, nb])
                total = total + inner[nb]
        total = total + 2.0
        for f in range(fields):
            a = adj[0, f, x]
            out = total * a
            for g in range(fields):
                out = out + coup[0, f, g] * adj[0, g, x]
            for (axis, shift, _), face in zip(shifts, faces):
                out = out - face * pltpu.roll(a, shift, axis)
            for nb, face in inner.items():
                out = out - face * adj[0, f, nb]
            res[0, f, x] = out

    cells = layers * ny
    for j in range(nodes // CHUNK):
        at = pl.ds(j * CHUNK, CHUNK)
        c = cell[:, at]
        row = (c // LANES) % groups * cells + c // nz
        count = groups * cells
        hot = (lax.broadcasted_iota(jnp.int32, (count, CHUNK), 0) == row).astype(F32).astype(BF16)
        pick_row[0:count, at] = hot
        pick_row[count:2 * count, at] = hot
        low = patch[:, at] % LANES
        hot = (lax.broadcasted_iota(jnp.int32, (LANES, CHUNK), 0) == low).astype(F32)
        pick_patch_t[at, :] = hot.T.astype(BF16)
        pick_patch[0:LANES, at] = hot.astype(BF16)
        pick_patch[LANES:2 * LANES, at] = hot.astype(BF16)
    normal8[...] = jnp.zeros_like(normal8)
    for h in range(halves):
        normal8[3 * h:3 * h + 3, :] = normal[...]

    @pl.when(uses_own)
    def _():
        own_morph.wait()

    @pl.when(gets_near)
    def _():
        near_morph.wait_recv()

    @pl.when(is_site)
    def _():
        m_hi, m_lo = parts(morph[...])
        morph_hi[...] = m_hi
        morph_lo[...] = m_lo

    @pl.when(has_before)
    def _():
        for copy in up:
            copy.wait_recv()

    @pl.when(has_after)
    def _():
        for copy in down:
            copy.wait_recv()

    cell_sens = []
    for x in range(layers):
        v = visc[0, x]
        acc = jnp.zeros_like(v)
        for f in range(fields):
            a = adj[0, f, x]
            r = res[0, f, x]
            if x == 0:
                r = r - 0.5 * (v + before_v[...]) * (before_a[f] - a)
            if x == layers - 1:
                r = r - 0.5 * (v + after_v[...]) * (after_a[f] - a)
            res[0, f, x] = r
            acc = acc + a * r
        cell_sens.append(weight[0] * v * acc)
    s = jnp.concatenate(cell_sens, axis=0)
    s = jnp.concatenate([s[:, g * LANES:(g + 1) * LANES] for g in range(groups)], axis=0)
    s = jnp.concatenate(parts(s.T), axis=1)

    owner_rows = n_space * rows
    shape3 = (n_space, rows, CHUNK)
    half_of = lax.broadcasted_iota(jnp.int32, shape3, 0) * halves + lax.broadcasted_iota(jnp.int32, shape3, 1) // 3
    sums_now = jnp.zeros((2 * owner_rows, LANES), F32)
    for j in range(nodes // CHUNK):
        at = pl.ds(j * CHUNK, CHUNK)
        t = dot(s, pick_row[:, at])
        lane = cell[:, at] % LANES
        here = lax.broadcasted_iota(jnp.int32, t.shape, 0) == lane
        sens = jnp.sum(jnp.where(here, t, 0.0), axis=0, keepdims=True)
        part = normal8[:, at] * sens
        high = patch[:, at] // LANES
        spread = jnp.where(half_of == high[None], part[None], 0.0).reshape(owner_rows, CHUNK)
        a = jnp.concatenate(parts(spread), axis=0)
        sums_now = sums_now + dot(a, pick_patch_t[at, :])
    dense[...] = (sums_now[:owner_rows] + sums_now[owner_rows:]).reshape(dense.shape)

    pair = lax.div(y0, 2)

    def owner_of(d):
        return lax.rem(mine + d, n_space)

    def to_site(q, d):
        owner = owner_of(d)
        odd = lax.rem(owner, 2)
        return pltpu.make_async_remote_copy(
            src_ref=dense.at[owner, 0:used], dst_ref=got.at[y0, s0, 0:used],
            send_sem=send1.at[q, d], recv_sem=recv1.at[y0, s0],
            device_id={"yaw": 2 * q + odd, "space": owner - odd + 1},
        )

    def from_slab(yaw, slab):
        return pltpu.make_async_remote_copy(
            src_ref=dense.at[0, 0:used], dst_ref=got.at[yaw, slab, 0:used],
            send_sem=send1.at[0, 0], recv_sem=recv1.at[yaw, slab], device_id={"yaw": yaw, "space": slab},
        )

    def sites(act):
        for q in range(n_yaw // 2):
            @pl.when(jnp.logical_not(jnp.logical_and(is_site, pair == q)))
            def _():
                act(to_site(q, 0))

            each(n_space, lambda d: act(to_site(q, d)))

    pl.semaphore_wait(row_in, n_yaw - 1)
    sites(lambda copy: copy.start())

    def to_slab(k, slab):
        return pltpu.make_async_remote_copy(
            src_ref=grads.at[mine, 0:used], dst_ref=grads.at[mine, 0:used],
            send_sem=send3.at[k, slab], recv_sem=recv3.at[mine],
            device_id={"yaw": 2 * pair + k, "space": slab},
        )

    def slabs(act):
        def one(slab):
            for k in range(2):
                @pl.when(jnp.logical_not(jnp.logical_and(slab == s0, turn == k)))
                def _():
                    act(to_slab(k, slab))

        each(n_space, one, 0)

    def from_owner(d):
        owner = owner_of(d)
        return pltpu.make_async_remote_copy(
            src_ref=grads.at[owner, 0:used], dst_ref=grads.at[owner, 0:used],
            send_sem=send3.at[0, 0], recv_sem=recv3.at[owner],
            device_id={"yaw": 2 * pair + lax.rem(owner, 2), "space": owner - lax.rem(owner, 2) + 1},
        )

    @pl.when(is_site)
    def _():
        got[y0, s0] = dense[mine]
        for dy in reversed(range(n_yaw)):
            each(n_space, lambda d: from_slab(yaw_peer(dy), space_peer(d)).wait_recv(), 0 if dy else 1)
        p = jnp.sum(jnp.sum(got[...], axis=0), axis=0)
        p = jnp.concatenate([p[3 * h:3 * h + 3] for h in range(halves)], axis=1)
        p = jnp.concatenate([p, jnp.zeros((5, owned), F32)], axis=0)
        hi, lo = parts(p)
        both = jnp.concatenate([hi.astype(F32), lo.astype(F32)], axis=0).astype(BF16)
        smooth = dot(both, morph_hi[...], ((1,), (1,))) + dot(both, morph_lo[...], ((1,), (1,)))
        g = p + smooth[0:8] + smooth[8:16]
        for h in range(halves):
            grads[mine, 3 * h:3 * h + 3] = g[0:3, h * LANES:(h + 1) * LANES]
        slabs(lambda copy: copy.start())

    @pl.when(jnp.logical_not(is_site))
    def _():
        from_owner(0).wait_recv()

    each(n_space, lambda d: from_owner(d).wait_recv())
    for h in range(halves):
        pgrad[:, h * LANES:(h + 1) * LANES] = grads[s0, 3 * h:3 * h + 3]
    grads_out[...] = grads[...]

    @pl.when(has_before)
    def _():
        for copy in down:
            copy.wait_send()

    @pl.when(has_after)
    def _():
        for copy in up:
            copy.wait_send()

    @pl.when(gives_near)
    def _():
        near_morph.wait_send()

    sites(lambda copy: copy.wait_send())

    @pl.when(is_site)
    def _():
        slabs(lambda copy: copy.wait_send())


def finish(res, pgrad, grads, patch, pick_patch, res_out, pgrad_out, ngrad_out, ngrad, sem):
    n_space, rows, _ = grads.shape
    nodes = patch.shape[1]
    halves = pgrad.shape[1] // LANES
    copies = [
        pltpu.make_async_copy(src, dst, sem.at[i])
        for i, (src, dst) in enumerate(((res, res_out), (pgrad, pgrad_out), (ngrad, ngrad_out)))
    ]
    for copy in copies[:2]:
        copy.start()
    shape3 = (n_space, rows, CHUNK)
    half_of = lax.broadcasted_iota(jnp.int32, shape3, 0) * halves + lax.broadcasted_iota(jnp.int32, shape3, 1) // 3
    allg = jnp.concatenate(parts(grads[...].reshape(n_space * rows, LANES)), axis=1)
    for j in range(nodes // CHUNK):
        at = pl.ds(j * CHUNK, CHUNK)
        e = dot(allg, pick_patch[:, at]).reshape(shape3)
        high = patch[:, at] // LANES
        e = jnp.sum(jnp.where(half_of == high[None], e, 0.0), axis=0)
        out = e[0:3]
        for h in range(1, halves):
            out = out + e[3 * h:3 * h + 3]
        ngrad[:, at] = out
    copies[2].start()
    for copy in copies:
        copy.wait()


def shards(
    n_yaw, n_space,
    adjoint, viscosity, coupling, yaw_weight, node_cell, node_patch, node_normal, morph_kernel,
):
    _, fields, layers, ny, nz = adjoint.shape
    nodes = node_cell.shape[0]
    owned = morph_kernel.shape[1]
    rows = -(-3 * (owned // LANES) // 8) * 8
    vmem = pl.BlockSpec(memory_space=pltpu.VMEM)
    anywhere = pl.BlockSpec(memory_space=pl.ANY)
    dma = pltpu.SemaphoreType.DMA
    outs = pl.pallas_call(
        functools.partial(kernel, n_yaw, n_space),
        out_shape=(
            pltpu.VMEM(adjoint.shape, F32),
            pltpu.VMEM((3, owned), F32),
            pltpu.VMEM((n_space, rows, LANES), F32),
            pltpu.VMEM((1, nodes), jnp.int32),
            pltpu.VMEM((2 * LANES, nodes), BF16),
        ),
        in_specs=[pl.BlockSpec(memory_space=pltpu.HBM)] * 8,
        out_specs=(vmem,) * 5,
        scratch_shapes=[
            pltpu.SMEM(coupling.shape, F32),
            pltpu.SMEM((1,), F32),
            pltpu.VMEM(adjoint.shape, F32),
            pltpu.VMEM(viscosity.shape, F32),
            pltpu.VMEM((1, nodes), jnp.int32),
            pltpu.VMEM(node_normal.shape, F32),
            pltpu.VMEM(morph_kernel.shape, F32),
            pltpu.VMEM((fields, ny, nz), F32),
            pltpu.VMEM((ny, nz), F32),
            pltpu.VMEM((fields, ny, nz), F32),
            pltpu.VMEM((ny, nz), F32),
            pltpu.VMEM((2 * layers * ny * nz // LANES, nodes), BF16),
            pltpu.VMEM((nodes, LANES), BF16),
            pltpu.VMEM((rows, nodes), F32),
            pltpu.VMEM((owned, owned), BF16),
            pltpu.VMEM((owned, owned), BF16),
            pltpu.VMEM((n_space, rows, LANES), F32),
            pltpu.VMEM((n_yaw, n_space, rows, LANES), F32),
            pltpu.VMEM((n_space, rows, LANES), F32),
            pltpu.SemaphoreType.REGULAR,
            dma((8,)), dma((4,)), dma((4,)),
            dma((n_yaw // 2, n_space)), dma((n_yaw, n_space)),
            dma((2, n_space)), dma((n_space,)), dma, dma,
        ],
        compiler_params=pltpu.CompilerParams(
            collective_id=0, has_side_effects=True, vmem_limit_bytes=56 * 1024 * 1024
        ),
        cost_estimate=pl.CostEstimate(flops=400_000_000, bytes_accessed=1_000_000, transcendentals=0),
    )(
        coupling, yaw_weight, adjoint, viscosity,
        node_cell[None], node_patch[None], node_normal, morph_kernel,
    )
    return pl.pallas_call(
        finish,
        out_shape=(
            jax.ShapeDtypeStruct(adjoint.shape, F32),
            jax.ShapeDtypeStruct((3, owned), F32),
            jax.ShapeDtypeStruct((3, nodes), F32),
        ),
        in_specs=[vmem] * 5,
        out_specs=(anywhere,) * 3,
        scratch_shapes=[pltpu.VMEM((3, nodes), F32), dma((3,))],
        compiler_params=pltpu.CompilerParams(vmem_limit_bytes=4 * 1024 * 1024),
    )(*outs)


def solution(mesh):
    return jax.shard_map(
        functools.partial(shards, mesh.shape["yaw"], mesh.shape["space"]),
        mesh=mesh,
        in_specs=(
            P("yaw", None, "space", None, None),
            P("yaw", "space", None, None),
            P("yaw", None, None),
            P("yaw"),
            P("space"),
            P("space"),
            P(None, "space"),
            P("space", None),
        ),
        out_specs=(P("yaw", None, "space", None, None), P(None, "space"), P(None, "space")),
        check_vma=False,
    )
```

```python
import functools

import jax
import jax.numpy as jnp
from jax import lax
from jax.experimental import pallas as pl
from jax.experimental.pallas import tpu as pltpu
from jax.sharding import PartitionSpec as P

LANES = 128
CHUNK = 256
F32 = jnp.float32
BF16 = jnp.bfloat16


def dot(a, b, contract=((1,), (0,))):
    return lax.dot_general(a, b, (contract, ((), ())), preferred_element_type=F32)


def parts(x):
    hi = x.astype(BF16)
    return hi, (x - hi.astype(F32)).astype(BF16)


def each(count, body, first=1):
    if count <= 8:
        for d in range(first, count):
            body(d)
    else:
        lax.fori_loop(first, count, lambda d, c: (body(d), c)[1], 0)


def kernel(
    n_yaw, n_space,
    coup_in, weight_in, adj_in, visc_in, cell_in, patch_in, normal_in, morph_in,
    res, pgrad, grads_out, patch, pick_patch,
    coup, weight, adj, visc, cell, normal, morph,
    before_a, before_v, after_a, after_v,
    pick_row, pick_patch_t, normal8, morph_hi, morph_lo,
    dense, got, grads,
    above_in, row_in, load, halo_send, halo_recv, send1, recv1, send3, recv3, morph_send, morph_recv,
):
    _, fields, layers, ny, nz = adj.shape
    nodes = cell.shape[1]
    owned = morph.shape[1]
    halves = owned // LANES
    used = 3 * halves
    rows = dense.shape[1]
    groups = nz // LANES
    y0, s0 = lax.axis_index("yaw"), lax.axis_index("space")

    def space_peer(d):
        return lax.rem(s0 + d, n_space)

    def yaw_peer(d):
        return lax.rem(y0 + d, n_yaw)

    has_before, has_after = s0 > 0, s0 < n_space - 1

    barrier = pltpu.get_barrier_semaphore()

    def enter(slab):
        pl.semaphore_signal(barrier, inc=1, device_id={"space": slab})

    pl.when(has_before)(lambda: enter(s0 - 1))
    pl.when(has_after)(lambda: enter(s0 + 1))
    loads = [
        pltpu.make_async_copy(src, dst, load.at[i])
        for i, (src, dst) in enumerate((
            (adj_in, adj), (visc_in, visc), (coup_in, coup), (cell_in, cell), (patch_in, patch),
            (normal_in, normal), (weight_in, weight),
        ))
    ]
    for copy in loads[:2]:
        copy.start()
    each(n_yaw, lambda d: pl.semaphore_signal(barrier, inc=1, device_id={"yaw": yaw_peer(d)}))
    each(n_space, lambda slab: pl.when(slab > s0 + 1)(lambda: enter(slab)), 2)
    for copy in loads[2:]:
        copy.start()
    grads[...] = jnp.zeros_like(grads)

    core = lax.rem(s0, 2)
    first = s0 - core
    turn = lax.rem(y0, 2)
    mine = first + turn
    is_site = core == 1
    own_morph = pltpu.make_async_copy(morph_in, morph, load.at[7])
    near_morph = pltpu.make_async_remote_copy(
        src_ref=morph_in, dst_ref=morph, send_sem=morph_send, recv_sem=morph_recv,
        device_id={"space": first + 1},
    )
    uses_own = jnp.logical_and(is_site, turn == 1)
    gets_near = jnp.logical_and(is_site, turn == 0)
    gives_near = jnp.logical_and(core == 0, turn == 0)

    @pl.when(uses_own)
    def _():
        own_morph.start()

    pl.semaphore_wait(barrier, s0 + has_after.astype(jnp.int32) + n_yaw - 1)

    def halo(slot, src, dst, peer):
        return pltpu.make_async_remote_copy(
            src_ref=src, dst_ref=dst, send_sem=halo_send.at[slot], recv_sem=halo_recv.at[slot],
            device_id={"space": peer},
        )

    up = (
        halo(0, adj.at[0, :, layers - 1], before_a, s0 + 1),
        halo(1, visc.at[0, layers - 1], before_v, s0 + 1),
    )
    down = (
        halo(2, adj_in.at[0, :, 0], after_a, s0 - 1),
        halo(3, visc_in.at[0, 0], after_v, s0 - 1),
    )

    @pl.when(has_before)
    def _():
        for copy in down:
            copy.start()

    for copy in loads[:2]:
        copy.wait()

    @pl.when(has_after)
    def _():
        for copy in up:
            copy.start()

    each(n_space - 2, lambda slab: pl.when(slab < s0 - 1)(
        lambda: pl.semaphore_signal(above_in, inc=1, device_id={"space": slab})
    ), 0)

    @pl.when(gives_near)
    def _():
        near_morph.start()

    @pl.when(jnp.logical_not(has_before))
    def _():
        before_a[...] = jnp.zeros_like(before_a)
        before_v[...] = jnp.zeros_like(before_v)

    @pl.when(jnp.logical_not(has_after))
    def _():
        after_a[...] = jnp.zeros_like(after_a)
        after_v[...] = jnp.zeros_like(after_v)

    for copy in loads[2:]:
        copy.wait()

    at_y = lax.broadcasted_iota(jnp.int32, (ny, nz), 0)
    at_z = lax.broadcasted_iota(jnp.int32, (ny, nz), 1)
    shifts = (
        (0, 1, at_y > 0), (0, ny - 1, at_y < ny - 1), (1, 1, at_z > 0), (1, nz - 1, at_z < nz - 1)
    )
    for x in range(layers):
        v = visc[0, x]
        total = jnp.zeros_like(v)
        faces = []
        for axis, shift, inside in shifts:
            face = 0.5 * (v + jnp.where(inside, pltpu.roll(v, shift, axis), 0.0))
            total = total + face
            faces.append(jnp.where(inside, face, 0.0))
        inner = {}
        for nb in (x - 1, x + 1):
            if 0 <= nb < layers:
                inner[nb] = 0.5 * (v + visc[0, nb])
                total = total + inner[nb]
        total = total + 2.0
        for f in range(fields):
            a = adj[0, f, x]
            out = total * a
            for g in range(fields):
                out = out + coup[0, f, g] * adj[0, g, x]
            for (axis, shift, _), face in zip(shifts, faces):
                out = out - face * pltpu.roll(a, shift, axis)
            for nb, face in inner.items():
                out = out - face * adj[0, f, nb]
            res[0, f, x] = out

    cells = layers * ny
    for j in range(nodes // CHUNK):
        at = pl.ds(j * CHUNK, CHUNK)
        c = cell[:, at]
        row = (c // LANES) % groups * cells + c // nz
        count = groups * cells
        hot = (lax.broadcasted_iota(jnp.int32, (count, CHUNK), 0) == row).astype(F32).astype(BF16)
        pick_row[0:count, at] = hot
        pick_row[count:2 * count, at] = hot
        low = patch[:, at] % LANES
        hot = (lax.broadcasted_iota(jnp.int32, (LANES, CHUNK), 0) == low).astype(F32)
        pick_patch_t[at, :] = hot.T.astype(BF16)
        pick_patch[0:LANES, at] = hot.astype(BF16)
        pick_patch[LANES:2 * LANES, at] = hot.astype(BF16)
    normal8[...] = jnp.zeros_like(normal8)
    for h in range(halves):
        normal8[3 * h:3 * h + 3, :] = normal[...]

    @pl.when(uses_own)
    def _():
        own_morph.wait()

    @pl.when(gets_near)
    def _():
        near_morph.wait_recv()

    @pl.when(is_site)
    def _():
        m_hi, m_lo = parts(morph[...])
        morph_hi[...] = m_hi
        morph_lo[...] = m_lo

    @pl.when(s0 < n_space - 2)
    def _():
        pl.semaphore_wait(above_in, n_space - 2 - s0)

    each(n_yaw, lambda d: pl.semaphore_signal(row_in, inc=1, device_id={"yaw": yaw_peer(d)}))

    @pl.when(has_before)
    def _():
        for copy in up:
            copy.wait_recv()

    @pl.when(has_after)
    def _():
        for copy in down:
            copy.wait_recv()

    cell_sens = []
    for x in range(layers):
        v = visc[0, x]
        acc = jnp.zeros_like(v)
        for f in range(fields):
            a = adj[0, f, x]
            r = res[0, f, x]
            if x == 0:
                r = r - 0.5 * (v + before_v[...]) * (before_a[f] - a)
            if x == layers - 1:
                r = r - 0.5 * (v + after_v[...]) * (after_a[f] - a)
            res[0, f, x] = r
            acc = acc + a * r
        cell_sens.append(weight[0] * v * acc)
    s = jnp.concatenate(cell_sens, axis=0)
    s = jnp.concatenate([s[:, g * LANES:(g + 1) * LANES] for g in range(groups)], axis=0)
    s = jnp.concatenate(parts(s.T), axis=1)

    owner_rows = n_space * rows
    shape3 = (n_space, rows, CHUNK)
    half_of = lax.broadcasted_iota(jnp.int32, shape3, 0) * halves + lax.broadcasted_iota(jnp.int32, shape3, 1) // 3
    sums_now = jnp.zeros((2 * owner_rows, LANES), F32)
    for j in range(nodes // CHUNK):
        at = pl.ds(j * CHUNK, CHUNK)
        t = dot(s, pick_row[:, at])
        lane = cell[:, at] % LANES
        here = lax.broadcasted_iota(jnp.int32, t.shape, 0) == lane
        sens = jnp.sum(jnp.where(here, t, 0.0), axis=0, keepdims=True)
        part = normal8[:, at] * sens
        high = patch[:, at] // LANES
        spread = jnp.where(half_of == high[None], part[None], 0.0).reshape(owner_rows, CHUNK)
        a = jnp.concatenate(parts(spread), axis=0)
        sums_now = sums_now + dot(a, pick_patch_t[at, :])
    dense[...] = (sums_now[:owner_rows] + sums_now[owner_rows:]).reshape(dense.shape)

    pair = lax.div(y0, 2)

    def owner_of(d):
        return lax.rem(mine + d, n_space)

    def to_site(q, d):
        owner = owner_of(d)
        odd = lax.rem(owner, 2)
        return pltpu.make_async_remote_copy(
            src_ref=dense.at[owner, 0:used], dst_ref=got.at[y0, s0, 0:used],
            send_sem=send1.at[q, d], recv_sem=recv1.at[y0, s0],
            device_id={"yaw": 2 * q + odd, "space": owner - odd + 1},
        )

    def from_slab(yaw, slab):
        return pltpu.make_async_remote_copy(
            src_ref=dense.at[0, 0:used], dst_ref=got.at[yaw, slab, 0:used],
            send_sem=send1.at[0, 0], recv_sem=recv1.at[yaw, slab], device_id={"yaw": yaw, "space": slab},
        )

    def sites(act):
        for q in range(n_yaw // 2):
            @pl.when(jnp.logical_not(jnp.logical_and(is_site, pair == q)))
            def _():
                act(to_site(q, 0))

            each(n_space, lambda d: act(to_site(q, d)))

    pl.semaphore_wait(row_in, n_yaw - 1)
    sites(lambda copy: copy.start())

    def to_slab(k, slab):
        return pltpu.make_async_remote_copy(
            src_ref=grads.at[mine, 0:used], dst_ref=grads.at[mine, 0:used],
            send_sem=send3.at[k, slab], recv_sem=recv3.at[mine],
            device_id={"yaw": 2 * pair + k, "space": slab},
        )

    def slabs(act):
        def one(slab):
            for k in range(2):
                @pl.when(jnp.logical_not(jnp.logical_and(slab == s0, turn == k)))
                def _():
                    act(to_slab(k, slab))

        each(n_space, one, 0)

    def from_owner(d):
        owner = owner_of(d)
        return pltpu.make_async_remote_copy(
            src_ref=grads.at[owner, 0:used], dst_ref=grads.at[owner, 0:used],
            send_sem=send3.at[0, 0], recv_sem=recv3.at[owner],
            device_id={"yaw": 2 * pair + lax.rem(owner, 2), "space": owner - lax.rem(owner, 2) + 1},
        )

    @pl.when(is_site)
    def _():
        got[y0, s0] = dense[mine]
        for dy in reversed(range(n_yaw)):
            each(n_space, lambda d: from_slab(yaw_peer(dy), space_peer(d)).wait_recv(), 0 if dy else 1)
        p = jnp.sum(jnp.sum(got[...], axis=0), axis=0)
        p = jnp.concatenate([p[3 * h:3 * h + 3] for h in range(halves)], axis=1)
        p = jnp.concatenate([p, jnp.zeros((5, owned), F32)], axis=0)
        hi, lo = parts(p)
        both = jnp.concatenate([hi.astype(F32), lo.astype(F32)], axis=0).astype(BF16)
        smooth = dot(both, morph_hi[...], ((1,), (1,))) + dot(both, morph_lo[...], ((1,), (1,)))
        g = p + smooth[0:8] + smooth[8:16]
        for h in range(halves):
            grads[mine, 3 * h:3 * h + 3] = g[0:3, h * LANES:(h + 1) * LANES]
        slabs(lambda copy: copy.start())

    @pl.when(jnp.logical_not(is_site))
    def _():
        from_owner(0).wait_recv()

    each(n_space, lambda d: from_owner(d).wait_recv())
    for h in range(halves):
        pgrad[:, h * LANES:(h + 1) * LANES] = grads[s0, 3 * h:3 * h + 3]
    grads_out[...] = grads[...]

    @pl.when(has_before)
    def _():
        for copy in down:
            copy.wait_send()

    @pl.when(has_after)
    def _():
        for copy in up:
            copy.wait_send()

    @pl.when(gives_near)
    def _():
        near_morph.wait_send()

    sites(lambda copy: copy.wait_send())

    @pl.when(is_site)
    def _():
        slabs(lambda copy: copy.wait_send())


def finish(res, pgrad, grads, patch, pick_patch, res_out, pgrad_out, ngrad_out, ngrad, sem):
    n_space, rows, _ = grads.shape
    nodes = patch.shape[1]
    halves = pgrad.shape[1] // LANES
    copies = [
        pltpu.make_async_copy(src, dst, sem.at[i])
        for i, (src, dst) in enumerate(((res, res_out), (pgrad, pgrad_out), (ngrad, ngrad_out)))
    ]
    for copy in copies[:2]:
        copy.start()
    shape3 = (n_space, rows, CHUNK)
    half_of = lax.broadcasted_iota(jnp.int32, shape3, 0) * halves + lax.broadcasted_iota(jnp.int32, shape3, 1) // 3
    allg = jnp.concatenate(parts(grads[...].reshape(n_space * rows, LANES)), axis=1)
    for j in range(nodes // CHUNK):
        at = pl.ds(j * CHUNK, CHUNK)
        e = dot(allg, pick_patch[:, at]).reshape(shape3)
        high = patch[:, at] // LANES
        e = jnp.sum(jnp.where(half_of == high[None], e, 0.0), axis=0)
        out = e[0:3]
        for h in range(1, halves):
            out = out + e[3 * h:3 * h + 3]
        ngrad[:, at] = out
    copies[2].start()
    for copy in copies:
        copy.wait()


def shards(
    n_yaw, n_space,
    adjoint, viscosity, coupling, yaw_weight, node_cell, node_patch, node_normal, morph_kernel,
):
    _, fields, layers, ny, nz = adjoint.shape
    nodes = node_cell.shape[0]
    owned = morph_kernel.shape[1]
    rows = -(-3 * (owned // LANES) // 8) * 8
    vmem = pl.BlockSpec(memory_space=pltpu.VMEM)
    anywhere = pl.BlockSpec(memory_space=pl.ANY)
    dma = pltpu.SemaphoreType.DMA
    outs = pl.pallas_call(
        functools.partial(kernel, n_yaw, n_space),
        out_shape=(
            pltpu.VMEM(adjoint.shape, F32),
            pltpu.VMEM((3, owned), F32),
            pltpu.VMEM((n_space, rows, LANES), F32),
            pltpu.VMEM((1, nodes), jnp.int32),
            pltpu.VMEM((2 * LANES, nodes), BF16),
        ),
        in_specs=[pl.BlockSpec(memory_space=pltpu.HBM)] * 8,
        out_specs=(vmem,) * 5,
        scratch_shapes=[
            pltpu.SMEM(coupling.shape, F32),
            pltpu.SMEM((1,), F32),
            pltpu.VMEM(adjoint.shape, F32),
            pltpu.VMEM(viscosity.shape, F32),
            pltpu.VMEM((1, nodes), jnp.int32),
            pltpu.VMEM(node_normal.shape, F32),
            pltpu.VMEM(morph_kernel.shape, F32),
            pltpu.VMEM((fields, ny, nz), F32),
            pltpu.VMEM((ny, nz), F32),
            pltpu.VMEM((fields, ny, nz), F32),
            pltpu.VMEM((ny, nz), F32),
            pltpu.VMEM((2 * layers * ny * nz // LANES, nodes), BF16),
            pltpu.VMEM((nodes, LANES), BF16),
            pltpu.VMEM((rows, nodes), F32),
            pltpu.VMEM((owned, owned), BF16),
            pltpu.VMEM((owned, owned), BF16),
            pltpu.VMEM((n_space, rows, LANES), F32),
            pltpu.VMEM((n_yaw, n_space, rows, LANES), F32),
            pltpu.VMEM((n_space, rows, LANES), F32),
            pltpu.SemaphoreType.REGULAR, pltpu.SemaphoreType.REGULAR,
            dma((8,)), dma((4,)), dma((4,)),
            dma((n_yaw // 2, n_space)), dma((n_yaw, n_space)),
            dma((2, n_space)), dma((n_space,)), dma, dma,
        ],
        compiler_params=pltpu.CompilerParams(
            collective_id=0, has_side_effects=True, vmem_limit_bytes=56 * 1024 * 1024
        ),
        cost_estimate=pl.CostEstimate(flops=400_000_000, bytes_accessed=1_000_000, transcendentals=0),
    )(
        coupling, yaw_weight, adjoint, viscosity,
        node_cell[None], node_patch[None], node_normal, morph_kernel,
    )
    return pl.pallas_call(
        finish,
        out_shape=(
            jax.ShapeDtypeStruct(adjoint.shape, F32),
            jax.ShapeDtypeStruct((3, owned), F32),
            jax.ShapeDtypeStruct((3, nodes), F32),
        ),
        in_specs=[vmem] * 5,
        out_specs=(anywhere,) * 3,
        scratch_shapes=[pltpu.VMEM((3, nodes), F32), dma((3,))],
        compiler_params=pltpu.CompilerParams(vmem_limit_bytes=4 * 1024 * 1024),
    )(*outs)


def solution(mesh):
    return jax.shard_map(
        functools.partial(shards, mesh.shape["yaw"], mesh.shape["space"]),
        mesh=mesh,
        in_specs=(
            P("yaw", None, "space", None, None),
            P("yaw", "space", None, None),
            P("yaw", None, None),
            P("yaw"),
            P("space"),
            P("space"),
            P(None, "space"),
            P("space", None),
        ),
        out_specs=(P("yaw", None, "space", None, None), P(None, "space"), P(None, "space")),
        check_vma=False,
    )
```

```python
import functools

import jax
import jax.numpy as jnp
from jax import lax
from jax.experimental import pallas as pl
from jax.experimental.pallas import tpu as pltpu
from jax.sharding import PartitionSpec as P

LANES = 128
CHUNK = 256
F32 = jnp.float32
BF16 = jnp.bfloat16


def dot(a, b, contract=((1,), (0,))):
    return lax.dot_general(a, b, (contract, ((), ())), preferred_element_type=F32)


def parts(x):
    hi = x.astype(BF16)
    return hi, (x - hi.astype(F32)).astype(BF16)


def each(count, body, first=1):
    if count <= 8:
        for d in range(first, count):
            body(d)
    else:
        lax.fori_loop(first, count, lambda d, c: (body(d), c)[1], 0)


def kernel(
    n_yaw, n_space,
    coup_in, weight_in, adj_in, visc_in, cell_in, patch_in, normal_in, morph_in,
    res, pgrad, grads_out, patch, pick_patch,
    coup, weight, adj, visc, cell, normal, morph,
    before_a, before_v, after_a, after_v,
    pick_row, pick_patch_t, normal8, morph_hi, morph_lo,
    dense, got, grads,
    row_in, all_in, load, halo_send, halo_recv, send1, recv1, send3, recv3, morph_send, morph_recv,
):
    _, fields, layers, ny, nz = adj.shape
    nodes = cell.shape[1]
    owned = morph.shape[1]
    halves = owned // LANES
    used = 3 * halves
    rows = dense.shape[1]
    groups = nz // LANES
    y0, s0 = lax.axis_index("yaw"), lax.axis_index("space")

    def space_peer(d):
        return lax.rem(s0 + d, n_space)

    def yaw_peer(d):
        return lax.rem(y0 + d, n_yaw)

    has_before, has_after = s0 > 0, s0 < n_space - 1
    last = jnp.logical_not(has_after)

    barrier = pltpu.get_barrier_semaphore()

    def enter(slab):
        pl.semaphore_signal(barrier, inc=1, device_id={"space": slab})

    pl.when(has_before)(lambda: enter(s0 - 1))
    pl.when(has_after)(lambda: enter(s0 + 1))
    loads = [
        pltpu.make_async_copy(src, dst, load.at[i])
        for i, (src, dst) in enumerate((
            (adj_in, adj), (visc_in, visc), (coup_in, coup), (cell_in, cell), (patch_in, patch),
            (normal_in, normal), (weight_in, weight),
        ))
    ]
    for copy in loads[:2]:
        copy.start()
    pl.when(last)(lambda: each(
        n_yaw, lambda d: pl.semaphore_signal(barrier, inc=1, device_id={"yaw": yaw_peer(d)})
    ))
    each(n_space, lambda slab: pl.when(slab > s0 + 1)(lambda: enter(slab)), 2)
    for copy in loads[2:]:
        copy.start()
    grads[...] = jnp.zeros_like(grads)

    core = lax.rem(s0, 2)
    first = s0 - core
    turn = lax.rem(y0, 2)
    mine = first + turn
    is_site = core == 1
    own_morph = pltpu.make_async_copy(morph_in, morph, load.at[7])
    near_morph = pltpu.make_async_remote_copy(
        src_ref=morph_in, dst_ref=morph, send_sem=morph_send, recv_sem=morph_recv,
        device_id={"space": first + 1},
    )
    uses_own = jnp.logical_and(is_site, turn == 1)
    gets_near = jnp.logical_and(is_site, turn == 0)
    gives_near = jnp.logical_and(core == 0, turn == 0)

    @pl.when(uses_own)
    def _():
        own_morph.start()

    pl.semaphore_wait(barrier, s0 + jnp.where(last, n_yaw - 1, 1))

    def halo(slot, src, dst, peer):
        return pltpu.make_async_remote_copy(
            src_ref=src, dst_ref=dst, send_sem=halo_send.at[slot], recv_sem=halo_recv.at[slot],
            device_id={"space": peer},
        )

    up = (
        halo(0, adj.at[0, :, layers - 1], before_a, s0 + 1),
        halo(1, visc.at[0, layers - 1], before_v, s0 + 1),
    )
    down = (
        halo(2, adj_in.at[0, :, 0], after_a, s0 - 1),
        halo(3, visc_in.at[0, 0], after_v, s0 - 1),
    )

    @pl.when(jnp.logical_and(has_before, core == 0))
    def _():
        for copy in down:
            copy.start()

    for copy in loads[:2]:
        copy.wait()

    @pl.when(has_after)
    def _():
        for copy in up:
            copy.start()

    @pl.when(core == 1)
    def _():
        for copy in down:
            copy.start()

    @pl.when(gives_near)
    def _():
        near_morph.start()

    @pl.when(last)
    def _():
        each(n_yaw, lambda d: pl.semaphore_signal(row_in, inc=1, device_id={"yaw": yaw_peer(d)}))
        pl.semaphore_wait(row_in, n_yaw - 1)
        each(n_space - 1, lambda slab: pl.semaphore_signal(all_in, inc=1, device_id={"space": slab}), 0)

    @pl.when(jnp.logical_not(has_before))
    def _():
        before_a[...] = jnp.zeros_like(before_a)
        before_v[...] = jnp.zeros_like(before_v)

    @pl.when(jnp.logical_not(has_after))
    def _():
        after_a[...] = jnp.zeros_like(after_a)
        after_v[...] = jnp.zeros_like(after_v)

    for copy in loads[2:]:
        copy.wait()

    at_y = lax.broadcasted_iota(jnp.int32, (ny, nz), 0)
    at_z = lax.broadcasted_iota(jnp.int32, (ny, nz), 1)
    shifts = (
        (0, 1, at_y > 0), (0, ny - 1, at_y < ny - 1), (1, 1, at_z > 0), (1, nz - 1, at_z < nz - 1)
    )
    for x in range(layers):
        v = visc[0, x]
        total = jnp.zeros_like(v)
        faces = []
        for axis, shift, inside in shifts:
            face = 0.5 * (v + jnp.where(inside, pltpu.roll(v, shift, axis), 0.0))
            total = total + face
            faces.append(jnp.where(inside, face, 0.0))
        inner = {}
        for nb in (x - 1, x + 1):
            if 0 <= nb < layers:
                inner[nb] = 0.5 * (v + visc[0, nb])
                total = total + inner[nb]
        total = total + 2.0
        for f in range(fields):
            a = adj[0, f, x]
            out = total * a
            for g in range(fields):
                out = out + coup[0, f, g] * adj[0, g, x]
            for (axis, shift, _), face in zip(shifts, faces):
                out = out - face * pltpu.roll(a, shift, axis)
            for nb, face in inner.items():
                out = out - face * adj[0, f, nb]
            res[0, f, x] = out

    cells = layers * ny
    for j in range(nodes // CHUNK):
        at = pl.ds(j * CHUNK, CHUNK)
        c = cell[:, at]
        row = (c // LANES) % groups * cells + c // nz
        count = groups * cells
        hot = (lax.broadcasted_iota(jnp.int32, (count, CHUNK), 0) == row).astype(F32).astype(BF16)
        pick_row[0:count, at] = hot
        pick_row[count:2 * count, at] = hot
        low = patch[:, at] % LANES
        hot = (lax.broadcasted_iota(jnp.int32, (LANES, CHUNK), 0) == low).astype(F32)
        pick_patch_t[at, :] = hot.T.astype(BF16)
        pick_patch[0:LANES, at] = hot.astype(BF16)
        pick_patch[LANES:2 * LANES, at] = hot.astype(BF16)
    normal8[...] = jnp.zeros_like(normal8)
    for h in range(halves):
        normal8[3 * h:3 * h + 3, :] = normal[...]

    @pl.when(uses_own)
    def _():
        own_morph.wait()

    @pl.when(gets_near)
    def _():
        near_morph.wait_recv()

    @pl.when(is_site)
    def _():
        m_hi, m_lo = parts(morph[...].T)
        morph_hi[...] = m_hi
        morph_lo[...] = m_lo

    @pl.when(has_before)
    def _():
        for copy in up:
            copy.wait_recv()

    @pl.when(has_after)
    def _():
        for copy in down:
            copy.wait_recv()

    cell_sens = []
    for x in range(layers):
        v = visc[0, x]
        acc = jnp.zeros_like(v)
        for f in range(fields):
            a = adj[0, f, x]
            r = res[0, f, x]
            if x == 0:
                r = r - 0.5 * (v + before_v[...]) * (before_a[f] - a)
            if x == layers - 1:
                r = r - 0.5 * (v + after_v[...]) * (after_a[f] - a)
            res[0, f, x] = r
            acc = acc + a * r
        cell_sens.append(weight[0] * v * acc)
    s = jnp.concatenate(cell_sens, axis=0)
    s = jnp.concatenate([s[:, g * LANES:(g + 1) * LANES] for g in range(groups)], axis=0)
    s = jnp.concatenate(parts(s.T), axis=1)

    owner_rows = n_space * rows
    shape3 = (n_space, rows, CHUNK)
    half_of = lax.broadcasted_iota(jnp.int32, shape3, 0) * halves + lax.broadcasted_iota(jnp.int32, shape3, 1) // 3
    sums_now = jnp.zeros((2 * owner_rows, LANES), F32)
    for j in range(nodes // CHUNK):
        at = pl.ds(j * CHUNK, CHUNK)
        t = dot(s, pick_row[:, at])
        lane = cell[:, at] % LANES
        here = lax.broadcasted_iota(jnp.int32, t.shape, 0) == lane
        sens = jnp.sum(jnp.where(here, t, 0.0), axis=0, keepdims=True)
        part = normal8[:, at] * sens
        high = patch[:, at] // LANES
        spread = jnp.where(half_of == high[None], part[None], 0.0).reshape(owner_rows, CHUNK)
        a = jnp.concatenate(parts(spread), axis=0)
        sums_now = sums_now + dot(a, pick_patch_t[at, :])
    dense[...] = (sums_now[:owner_rows] + sums_now[owner_rows:]).reshape(dense.shape)

    pair = lax.div(y0, 2)

    def owner_of(d):
        return lax.rem(mine + d, n_space)

    def slot(yaw, slab):
        return lax.rem(y0 - yaw + n_yaw, n_yaw) * n_space + lax.rem(s0 - slab + n_space, n_space)

    def wait_blocks(sem, start, count):
        blocks = got.at[start:start + count, 0:used]
        pltpu.make_async_copy(blocks, blocks, sem).wait()

    def to_site(q, d):
        owner = owner_of(d)
        odd = lax.rem(owner, 2)
        return pltpu.make_async_remote_copy(
            src_ref=dense.at[owner, 0:used],
            dst_ref=got.at[slot(2 * q + odd, owner - odd + 1), 0:used],
            send_sem=send1, recv_sem=recv1,
            device_id={"yaw": 2 * q + odd, "space": owner - odd + 1},
        )

    pl.when(has_after)(lambda: pl.semaphore_wait(all_in, 1))
    for q in range(n_yaw // 2):
        @pl.when(jnp.logical_not(jnp.logical_and(is_site, pair == q)))
        def _():
            to_site(q, 0).start()

        each(n_space, lambda d: to_site(q, d).start())

    def to_slab(k, slab):
        return pltpu.make_async_remote_copy(
            src_ref=grads.at[mine, 0:used], dst_ref=grads.at[mine, 0:used],
            send_sem=send3, recv_sem=recv3,
            device_id={"yaw": 2 * pair + k, "space": slab},
        )

    def to_slabs(slab):
        for k in range(2):
            @pl.when(jnp.logical_not(jnp.logical_and(slab == s0, turn == k)))
            def _():
                to_slab(k, slab).start()

    @pl.when(is_site)
    def _():
        got[0] = dense[mine]
        wait_blocks(recv1, 1, n_yaw * n_space - 1)
        p = jnp.sum(got[...], axis=0)
        p = jnp.concatenate([p[3 * h:3 * h + 3] for h in range(halves)], axis=1)
        p = jnp.concatenate([p, jnp.zeros((5, owned), F32)], axis=0)
        hi, lo = parts(p)
        both = jnp.concatenate([hi.astype(F32), lo.astype(F32)], axis=0).astype(BF16)
        smooth = dot(both, morph_hi[...]) + dot(both, morph_lo[...])
        g = p + smooth[0:8] + smooth[8:16]
        for h in range(halves):
            grads[mine, 3 * h:3 * h + 3] = g[0:3, h * LANES:(h + 1) * LANES]
        each(n_space, to_slabs, 0)

    @pl.when(has_before)
    def _():
        for copy in down:
            copy.wait_send()

    @pl.when(has_after)
    def _():
        for copy in up:
            copy.wait_send()

    @pl.when(gives_near)
    def _():
        near_morph.wait_send()

    sent = n_yaw // 2 * n_space

    @pl.when(is_site)
    def _():
        wait_blocks(send1, 0, sent - 1)
        wait_blocks(recv3, 0, n_space - 1)

    @pl.when(jnp.logical_not(is_site))
    def _():
        wait_blocks(send1, 0, sent)
        wait_blocks(recv3, 0, n_space)

    for h in range(halves):
        pgrad[:, h * LANES:(h + 1) * LANES] = grads[s0, 3 * h:3 * h + 3]
    grads_out[...] = grads[...]

    @pl.when(is_site)
    def _():
        wait_blocks(send3, 0, 2 * n_space - 1)


def finish(res, pgrad, grads, patch, pick_patch, res_out, pgrad_out, ngrad_out, ngrad, sem):
    n_space, rows, _ = grads.shape
    nodes = patch.shape[1]
    halves = pgrad.shape[1] // LANES
    copies = [
        pltpu.make_async_copy(src, dst, sem.at[i])
        for i, (src, dst) in enumerate(((res, res_out), (pgrad, pgrad_out), (ngrad, ngrad_out)))
    ]
    for copy in copies[:2]:
        copy.start()
    shape3 = (n_space, rows, CHUNK)
    half_of = lax.broadcasted_iota(jnp.int32, shape3, 0) * halves + lax.broadcasted_iota(jnp.int32, shape3, 1) // 3
    allg = jnp.concatenate(parts(grads[...].reshape(n_space * rows, LANES)), axis=1)
    for j in range(nodes // CHUNK):
        at = pl.ds(j * CHUNK, CHUNK)
        e = dot(allg, pick_patch[:, at]).reshape(shape3)
        high = patch[:, at] // LANES
        e = jnp.sum(jnp.where(half_of == high[None], e, 0.0), axis=0)
        out = e[0:3]
        for h in range(1, halves):
            out = out + e[3 * h:3 * h + 3]
        ngrad[:, at] = out
    copies[2].start()
    for copy in copies:
        copy.wait()


def shards(
    n_yaw, n_space,
    adjoint, viscosity, coupling, yaw_weight, node_cell, node_patch, node_normal, morph_kernel,
):
    _, fields, layers, ny, nz = adjoint.shape
    nodes = node_cell.shape[0]
    owned = morph_kernel.shape[1]
    rows = -(-3 * (owned // LANES) // 8) * 8
    vmem = pl.BlockSpec(memory_space=pltpu.VMEM)
    anywhere = pl.BlockSpec(memory_space=pl.ANY)
    dma = pltpu.SemaphoreType.DMA
    outs = pl.pallas_call(
        functools.partial(kernel, n_yaw, n_space),
        out_shape=(
            pltpu.VMEM(adjoint.shape, F32),
            pltpu.VMEM((3, owned), F32),
            pltpu.VMEM((n_space, rows, LANES), F32),
            pltpu.VMEM((1, nodes), jnp.int32),
            pltpu.VMEM((2 * LANES, nodes), BF16),
        ),
        in_specs=[pl.BlockSpec(memory_space=pltpu.HBM)] * 8,
        out_specs=(vmem,) * 5,
        scratch_shapes=[
            pltpu.SMEM(coupling.shape, F32),
            pltpu.SMEM((1,), F32),
            pltpu.VMEM(adjoint.shape, F32),
            pltpu.VMEM(viscosity.shape, F32),
            pltpu.VMEM((1, nodes), jnp.int32),
            pltpu.VMEM(node_normal.shape, F32),
            pltpu.VMEM(morph_kernel.shape, F32),
            pltpu.VMEM((fields, ny, nz), F32),
            pltpu.VMEM((ny, nz), F32),
            pltpu.VMEM((fields, ny, nz), F32),
            pltpu.VMEM((ny, nz), F32),
            pltpu.VMEM((2 * layers * ny * nz // LANES, nodes), BF16),
            pltpu.VMEM((nodes, LANES), BF16),
            pltpu.VMEM((rows, nodes), F32),
            pltpu.VMEM((owned, owned), BF16),
            pltpu.VMEM((owned, owned), BF16),
            pltpu.VMEM((n_space, rows, LANES), F32),
            pltpu.VMEM((n_yaw * n_space, rows, LANES), F32),
            pltpu.VMEM((n_space, rows, LANES), F32),
            pltpu.SemaphoreType.REGULAR, pltpu.SemaphoreType.REGULAR,
            dma((8,)), dma((4,)), dma((4,)),
            dma, dma, dma, dma, dma, dma,
        ],
        compiler_params=pltpu.CompilerParams(
            collective_id=0, has_side_effects=True, vmem_limit_bytes=56 * 1024 * 1024
        ),
        cost_estimate=pl.CostEstimate(flops=400_000_000, bytes_accessed=1_000_000, transcendentals=0),
    )(
        coupling, yaw_weight, adjoint, viscosity,
        node_cell[None], node_patch[None], node_normal, morph_kernel,
    )
    return pl.pallas_call(
        finish,
        out_shape=(
            jax.ShapeDtypeStruct(adjoint.shape, F32),
            jax.ShapeDtypeStruct((3, owned), F32),
            jax.ShapeDtypeStruct((3, nodes), F32),
        ),
        in_specs=[vmem] * 5,
        out_specs=(anywhere,) * 3,
        scratch_shapes=[pltpu.VMEM((3, nodes), F32), dma((3,))],
        compiler_params=pltpu.CompilerParams(vmem_limit_bytes=4 * 1024 * 1024),
    )(*outs)


def solution(mesh):
    return jax.shard_map(
        functools.partial(shards, mesh.shape["yaw"], mesh.shape["space"]),
        mesh=mesh,
        in_specs=(
            P("yaw", None, "space", None, None),
            P("yaw", "space", None, None),
            P("yaw", None, None),
            P("yaw"),
            P("space"),
            P("space"),
            P(None, "space"),
            P("space", None),
        ),
        out_specs=(P("yaw", None, "space", None, None), P(None, "space"), P(None, "space")),
        check_vma=False,
    )
```

```python
import functools

import jax
import jax.numpy as jnp
from jax import lax
from jax.experimental import pallas as pl
from jax.experimental.pallas import tpu as pltpu
from jax.sharding import PartitionSpec as P

LANES = 128
CHUNK = 256
WIDE = 1024
F32 = jnp.float32
BF16 = jnp.bfloat16


def dot(a, b, contract=((1,), (0,))):
    return lax.dot_general(a, b, (contract, ((), ())), preferred_element_type=F32)


def parts(x):
    hi = x.astype(BF16)
    return hi, (x - hi.astype(F32)).astype(BF16)


def each(count, body, first=1):
    if count <= 8:
        for d in range(first, count):
            body(d)
    else:
        lax.fori_loop(first, count, lambda d, c: (body(d), c)[1], 0)


def kernel(
    n_yaw, n_space,
    coup_in, weight_in, adj_in, visc_in, cell_in, patch_in, normal_in, morph_in,
    res, pgrad, grads_out, patch, pick_patch,
    coup, weight, adj, visc, cell, normal, morph,
    before_a, before_v, after_a, after_v,
    pick_row, pick_patch_t, normal8, morph_hi, morph_lo,
    inner_sens, dense, got, grads,
    row_in, all_in, load, halo_send, halo_recv, send1, recv1, send3, recv3, morph_send, morph_recv,
):
    _, fields, layers, ny, nz = adj.shape
    nodes = cell.shape[1]
    owned = morph.shape[1]
    halves = owned // LANES
    used = 3 * halves
    rows = dense.shape[1]
    groups = nz // LANES
    y0, s0 = lax.axis_index("yaw"), lax.axis_index("space")

    def space_peer(d):
        return lax.rem(s0 + d, n_space)

    def yaw_peer(d):
        return lax.rem(y0 + d, n_yaw)

    has_before, has_after = s0 > 0, s0 < n_space - 1
    last = jnp.logical_not(has_after)

    barrier = pltpu.get_barrier_semaphore()

    def enter(slab):
        pl.semaphore_signal(barrier, inc=1, device_id={"space": slab})

    pl.when(has_before)(lambda: enter(s0 - 1))
    pl.when(has_after)(lambda: enter(s0 + 1))
    loads = [
        pltpu.make_async_copy(src, dst, load.at[i])
        for i, (src, dst) in enumerate((
            (adj_in, adj), (visc_in, visc), (coup_in, coup), (cell_in, cell), (patch_in, patch),
            (normal_in, normal), (weight_in, weight),
        ))
    ]
    for copy in loads[:2]:
        copy.start()
    pl.when(last)(lambda: each(
        n_yaw, lambda d: pl.semaphore_signal(barrier, inc=1, device_id={"yaw": yaw_peer(d)})
    ))
    each(n_space, lambda slab: pl.when(slab > s0 + 1)(lambda: enter(slab)), 2)
    for copy in loads[2:]:
        copy.start()
    grads[...] = jnp.zeros_like(grads)

    core = lax.rem(s0, 2)
    first = s0 - core
    turn = lax.rem(y0, 2)
    mine = first + turn
    is_site = core == 1
    own_morph = pltpu.make_async_copy(morph_in, morph, load.at[7])
    near_morph = pltpu.make_async_remote_copy(
        src_ref=morph_in, dst_ref=morph, send_sem=morph_send, recv_sem=morph_recv,
        device_id={"space": first + 1},
    )
    uses_own = jnp.logical_and(is_site, turn == 1)
    gets_near = jnp.logical_and(is_site, turn == 0)
    gives_near = jnp.logical_and(core == 0, turn == 0)

    @pl.when(uses_own)
    def _():
        own_morph.start()

    pl.semaphore_wait(barrier, s0 + jnp.where(last, n_yaw - 1, 1))

    def halo(slot, src, dst, peer):
        return pltpu.make_async_remote_copy(
            src_ref=src, dst_ref=dst, send_sem=halo_send.at[slot], recv_sem=halo_recv.at[slot],
            device_id={"space": peer},
        )

    up = (
        halo(0, adj.at[0, :, layers - 1], before_a, s0 + 1),
        halo(1, visc.at[0, layers - 1], before_v, s0 + 1),
    )
    down = (
        halo(2, adj_in.at[0, :, 0], after_a, s0 - 1),
        halo(3, visc_in.at[0, 0], after_v, s0 - 1),
    )

    @pl.when(jnp.logical_and(has_before, core == 0))
    def _():
        for copy in down:
            copy.start()

    for copy in loads[:2]:
        copy.wait()

    @pl.when(has_after)
    def _():
        for copy in up:
            copy.start()

    @pl.when(core == 1)
    def _():
        for copy in down:
            copy.start()

    @pl.when(gives_near)
    def _():
        near_morph.start()

    @pl.when(last)
    def _():
        each(n_yaw, lambda d: pl.semaphore_signal(row_in, inc=1, device_id={"yaw": yaw_peer(d)}))
        pl.semaphore_wait(row_in, n_yaw - 1)
        each(n_space - 1, lambda slab: pl.semaphore_signal(all_in, inc=1, device_id={"space": slab}), 0)

    @pl.when(jnp.logical_not(has_before))
    def _():
        before_a[...] = jnp.zeros_like(before_a)
        before_v[...] = jnp.zeros_like(before_v)

    @pl.when(jnp.logical_not(has_after))
    def _():
        after_a[...] = jnp.zeros_like(after_a)
        after_v[...] = jnp.zeros_like(after_v)

    for copy in loads[2:]:
        copy.wait()

    at_y = lax.broadcasted_iota(jnp.int32, (ny, nz), 0)
    at_z = lax.broadcasted_iota(jnp.int32, (ny, nz), 1)
    shifts = (
        (0, 1, at_y > 0), (0, ny - 1, at_y < ny - 1), (1, 1, at_z > 0), (1, nz - 1, at_z < nz - 1)
    )
    for x in range(layers):
        v = visc[0, x]
        total = jnp.zeros_like(v)
        faces = []
        for axis, shift, inside in shifts:
            face = 0.5 * (v + jnp.where(inside, pltpu.roll(v, shift, axis), 0.0))
            total = total + face
            faces.append(jnp.where(inside, face, 0.0))
        inner = {}
        for nb in (x - 1, x + 1):
            if 0 <= nb < layers:
                inner[nb] = 0.5 * (v + visc[0, nb])
                total = total + inner[nb]
        total = total + 2.0
        acc = jnp.zeros_like(v)
        for f in range(fields):
            a = adj[0, f, x]
            out = total * a
            for g in range(fields):
                out = out + coup[0, f, g] * adj[0, g, x]
            for (axis, shift, _), face in zip(shifts, faces):
                out = out - face * pltpu.roll(a, shift, axis)
            for nb, face in inner.items():
                out = out - face * adj[0, f, nb]
            res[0, f, x] = out
            acc = acc + a * out
        inner_sens[x] = acc

    cells = layers * ny
    for j in range(nodes // CHUNK):
        at = pl.ds(j * CHUNK, CHUNK)
        c = cell[:, at]
        row = (c // LANES) % groups * cells + c // nz
        count = groups * cells
        hot = (lax.broadcasted_iota(jnp.int32, (count, CHUNK), 0) == row).astype(F32).astype(BF16)
        pick_row[0:count, at] = hot
        pick_row[count:2 * count, at] = hot
        low = patch[:, at] % LANES
        hot = (lax.broadcasted_iota(jnp.int32, (LANES, CHUNK), 0) == low).astype(F32)
        pick_patch_t[at, :] = hot.T.astype(BF16)
        pick_patch[0:LANES, at] = hot.astype(BF16)
        pick_patch[LANES:2 * LANES, at] = hot.astype(BF16)
    normal8[...] = jnp.zeros_like(normal8)
    for h in range(halves):
        normal8[3 * h:3 * h + 3, :] = normal[...]

    @pl.when(uses_own)
    def _():
        own_morph.wait()

    @pl.when(gets_near)
    def _():
        near_morph.wait_recv()

    @pl.when(is_site)
    def _():
        m_hi, m_lo = parts(morph[...].T)
        morph_hi[...] = m_hi
        morph_lo[...] = m_lo

    @pl.when(has_before)
    def _():
        for copy in up:
            copy.wait_recv()

    @pl.when(has_after)
    def _():
        for copy in down:
            copy.wait_recv()

    def outer(x):
        return [(before_a, before_v)] * (x == 0) + [(after_a, after_v)] * (x == layers - 1)

    cell_sens = []
    for x in range(layers):
        v = visc[0, x]
        acc = inner_sens[x]
        for far_a, far_v in outer(x):
            across = jnp.zeros_like(v)
            for f in range(fields):
                a = adj[0, f, x]
                across = across + a * (far_a[f] - a)
            acc = acc - 0.5 * (v + far_v[...]) * across
        cell_sens.append(weight[0] * v * acc)
    s = jnp.concatenate(cell_sens, axis=0)
    s = jnp.concatenate([s[:, g * LANES:(g + 1) * LANES] for g in range(groups)], axis=0)
    s = jnp.concatenate(parts(s.T), axis=1)

    owner_rows = n_space * rows
    wide = WIDE if nodes % WIDE == 0 else CHUNK
    shape3 = (n_space, rows, wide)
    half_of = lax.broadcasted_iota(jnp.int32, shape3, 0) * halves + lax.broadcasted_iota(jnp.int32, shape3, 1) // 3
    sums_now = jnp.zeros((2 * owner_rows, LANES), F32)
    for j in range(nodes // wide):
        at = pl.ds(j * wide, wide)
        t = dot(s, pick_row[:, at])
        lane = cell[:, at] % LANES
        here = lax.broadcasted_iota(jnp.int32, t.shape, 0) == lane
        sens = jnp.sum(jnp.where(here, t, 0.0), axis=0, keepdims=True)
        part = normal8[:, at] * sens
        hi = part.astype(BF16).astype(F32)
        chosen = half_of == (patch[:, at] // LANES)[None]
        a = jnp.concatenate([
            jnp.where(chosen, piece[None], 0.0).reshape(owner_rows, wide).astype(BF16) for piece in (hi, part - hi)
        ], axis=0)
        sums_now = sums_now + dot(a, pick_patch_t[at, :])
    dense[...] = (sums_now[:owner_rows] + sums_now[owner_rows:]).reshape(dense.shape)

    pair = lax.div(y0, 2)

    def owner_of(d):
        return lax.rem(mine + d, n_space)

    def slot(yaw, slab):
        return lax.rem(y0 - yaw + n_yaw, n_yaw) * n_space + lax.rem(s0 - slab + n_space, n_space)

    def wait_blocks(sem, start, count):
        blocks = got.at[start:start + count, 0:used]
        pltpu.make_async_copy(blocks, blocks, sem).wait()

    def to_site(q, d):
        owner = owner_of(d)
        odd = lax.rem(owner, 2)
        return pltpu.make_async_remote_copy(
            src_ref=dense.at[owner, 0:used],
            dst_ref=got.at[slot(2 * q + odd, owner - odd + 1), 0:used],
            send_sem=send1, recv_sem=recv1,
            device_id={"yaw": 2 * q + odd, "space": owner - odd + 1},
        )

    pl.when(has_after)(lambda: pl.semaphore_wait(all_in, 1))
    for q in range(n_yaw // 2):
        @pl.when(jnp.logical_not(jnp.logical_and(is_site, pair == q)))
        def _():
            to_site(q, 0).start()

        each(n_space, lambda d: to_site(q, d).start())

    for x in range(layers):
        v = visc[0, x]
        for far_a, far_v in outer(x):
            face = 0.5 * (v + far_v[...])
            for f in range(fields):
                res[0, f, x] = res[0, f, x] - face * (far_a[f] - adj[0, f, x])

    def to_slab(k, slab):
        return pltpu.make_async_remote_copy(
            src_ref=grads.at[mine, 0:used], dst_ref=grads.at[mine, 0:used],
            send_sem=send3, recv_sem=recv3,
            device_id={"yaw": 2 * pair + k, "space": slab},
        )

    def to_slabs(slab):
        for k in range(2):
            @pl.when(jnp.logical_not(jnp.logical_and(slab == s0, turn == k)))
            def _():
                to_slab(k, slab).start()

    @pl.when(is_site)
    def _():
        got[0] = dense[mine]
        wait_blocks(recv1, 1, n_yaw * n_space - 1)
        p = jnp.sum(got[...], axis=0)
        p = jnp.concatenate([p[3 * h:3 * h + 3] for h in range(halves)], axis=1)
        p = jnp.concatenate([p, jnp.zeros((5, owned), F32)], axis=0)
        hi, lo = parts(p)
        both = jnp.concatenate([hi.astype(F32), lo.astype(F32)], axis=0).astype(BF16)
        smooth = dot(both, morph_hi[...]) + dot(both, morph_lo[...])
        g = p + smooth[0:8] + smooth[8:16]
        for h in range(halves):
            grads[mine, 3 * h:3 * h + 3] = g[0:3, h * LANES:(h + 1) * LANES]
        each(n_space, to_slabs, 0)

    @pl.when(has_before)
    def _():
        for copy in down:
            copy.wait_send()

    @pl.when(has_after)
    def _():
        for copy in up:
            copy.wait_send()

    @pl.when(gives_near)
    def _():
        near_morph.wait_send()

    sent = n_yaw // 2 * n_space

    @pl.when(is_site)
    def _():
        wait_blocks(send1, 0, sent - 1)
        wait_blocks(recv3, 0, n_space - 1)

    @pl.when(jnp.logical_not(is_site))
    def _():
        wait_blocks(send1, 0, sent)
        wait_blocks(recv3, 0, n_space)

    for h in range(halves):
        pgrad[:, h * LANES:(h + 1) * LANES] = grads[s0, 3 * h:3 * h + 3]
    grads_out[...] = grads[...]

    @pl.when(is_site)
    def _():
        wait_blocks(send3, 0, 2 * n_space - 1)


def finish(res, pgrad, grads, patch, pick_patch, res_out, pgrad_out, ngrad_out, ngrad, sem):
    n_space, rows, _ = grads.shape
    nodes = patch.shape[1]
    halves = pgrad.shape[1] // LANES
    copies = [
        pltpu.make_async_copy(src, dst, sem.at[i])
        for i, (src, dst) in enumerate(((res, res_out), (pgrad, pgrad_out), (ngrad, ngrad_out)))
    ]
    for copy in copies[:2]:
        copy.start()
    shape3 = (n_space, rows, CHUNK)
    half_of = lax.broadcasted_iota(jnp.int32, shape3, 0) * halves + lax.broadcasted_iota(jnp.int32, shape3, 1) // 3
    allg = jnp.concatenate(parts(grads[...].reshape(n_space * rows, LANES)), axis=1)
    for j in range(nodes // CHUNK):
        at = pl.ds(j * CHUNK, CHUNK)
        e = dot(allg, pick_patch[:, at]).reshape(shape3)
        high = patch[:, at] // LANES
        e = jnp.sum(jnp.where(half_of == high[None], e, 0.0), axis=0)
        out = e[0:3]
        for h in range(1, halves):
            out = out + e[3 * h:3 * h + 3]
        ngrad[:, at] = out
    copies[2].start()
    for copy in copies:
        copy.wait()


def shards(
    n_yaw, n_space,
    adjoint, viscosity, coupling, yaw_weight, node_cell, node_patch, node_normal, morph_kernel,
):
    _, fields, layers, ny, nz = adjoint.shape
    nodes = node_cell.shape[0]
    owned = morph_kernel.shape[1]
    rows = -(-3 * (owned // LANES) // 8) * 8
    vmem = pl.BlockSpec(memory_space=pltpu.VMEM)
    anywhere = pl.BlockSpec(memory_space=pl.ANY)
    dma = pltpu.SemaphoreType.DMA
    outs = pl.pallas_call(
        functools.partial(kernel, n_yaw, n_space),
        out_shape=(
            pltpu.VMEM(adjoint.shape, F32),
            pltpu.VMEM((3, owned), F32),
            pltpu.VMEM((n_space, rows, LANES), F32),
            pltpu.VMEM((1, nodes), jnp.int32),
            pltpu.VMEM((2 * LANES, nodes), BF16),
        ),
        in_specs=[pl.BlockSpec(memory_space=pltpu.HBM)] * 8,
        out_specs=(vmem,) * 5,
        scratch_shapes=[
            pltpu.SMEM(coupling.shape, F32),
            pltpu.SMEM((1,), F32),
            pltpu.VMEM(adjoint.shape, F32),
            pltpu.VMEM(viscosity.shape, F32),
            pltpu.VMEM((1, nodes), jnp.int32),
            pltpu.VMEM(node_normal.shape, F32),
            pltpu.VMEM(morph_kernel.shape, F32),
            pltpu.VMEM((fields, ny, nz), F32),
            pltpu.VMEM((ny, nz), F32),
            pltpu.VMEM((fields, ny, nz), F32),
            pltpu.VMEM((ny, nz), F32),
            pltpu.VMEM((2 * layers * ny * nz // LANES, nodes), BF16),
            pltpu.VMEM((nodes, LANES), BF16),
            pltpu.VMEM((rows, nodes), F32),
            pltpu.VMEM((owned, owned), BF16),
            pltpu.VMEM((owned, owned), BF16),
            pltpu.VMEM((layers, ny, nz), F32),
            pltpu.VMEM((n_space, rows, LANES), F32),
            pltpu.VMEM((n_yaw * n_space, rows, LANES), F32),
            pltpu.VMEM((n_space, rows, LANES), F32),
            pltpu.SemaphoreType.REGULAR, pltpu.SemaphoreType.REGULAR,
            dma((8,)), dma((4,)), dma((4,)),
            dma, dma, dma, dma, dma, dma,
        ],
        compiler_params=pltpu.CompilerParams(
            collective_id=0, has_side_effects=True, vmem_limit_bytes=56 * 1024 * 1024
        ),
        cost_estimate=pl.CostEstimate(flops=400_000_000, bytes_accessed=1_000_000, transcendentals=0),
    )(
        coupling, yaw_weight, adjoint, viscosity,
        node_cell[None], node_patch[None], node_normal, morph_kernel,
    )
    return pl.pallas_call(
        finish,
        out_shape=(
            jax.ShapeDtypeStruct(adjoint.shape, F32),
            jax.ShapeDtypeStruct((3, owned), F32),
            jax.ShapeDtypeStruct((3, nodes), F32),
        ),
        in_specs=[vmem] * 5,
        out_specs=(anywhere,) * 3,
        scratch_shapes=[pltpu.VMEM((3, nodes), F32), dma((3,))],
        compiler_params=pltpu.CompilerParams(vmem_limit_bytes=4 * 1024 * 1024),
    )(*outs)


def solution(mesh):
    return jax.shard_map(
        functools.partial(shards, mesh.shape["yaw"], mesh.shape["space"]),
        mesh=mesh,
        in_specs=(
            P("yaw", None, "space", None, None),
            P("yaw", "space", None, None),
            P("yaw", None, None),
            P("yaw"),
            P("space"),
            P("space"),
            P(None, "space"),
            P("space", None),
        ),
        out_specs=(P("yaw", None, "space", None, None), P(None, "space"), P(None, "space")),
        check_vma=False,
    )
```

```python
import functools

import jax
import jax.numpy as jnp
from jax import lax
from jax.experimental import pallas as pl
from jax.experimental.pallas import tpu as pltpu
from jax.sharding import PartitionSpec as P

LANES = 128
CHUNK = 256
WIDE = 1024
F32 = jnp.float32
BF16 = jnp.bfloat16


def dot(a, b, contract=((1,), (0,))):
    return lax.dot_general(a, b, (contract, ((), ())), preferred_element_type=F32)


def parts(x):
    hi = x.astype(BF16)
    return hi, (x - hi.astype(F32)).astype(BF16)


def each(count, body, first=1):
    if count <= 8:
        for d in range(first, count):
            body(d)
    else:
        lax.fori_loop(first, count, lambda d, c: (body(d), c)[1], 0)


def kernel(
    n_yaw, n_space,
    coup_in, weight_in, adj_in, visc_in, cell_in, patch_in, tile_in, normal_in, morph_in,
    res, pgrad, grads_out, tile,
    coup, weight, adj, visc, cell, patch, normal, morph,
    before_a, before_v, after_a, after_v,
    pick_row, pick_patch_t, normal8, morph_hi, morph_lo,
    inner_sens, dense, got, grads,
    row_in, all_in, load, halo_send, halo_recv, send1, recv1, send3, recv3, morph_send, morph_recv,
):
    _, fields, layers, ny, nz = adj.shape
    nodes = cell.shape[1]
    owned = morph.shape[1]
    halves = owned // LANES
    used = 3 * halves
    rows = dense.shape[1]
    groups = nz // LANES
    y0, s0 = lax.axis_index("yaw"), lax.axis_index("space")

    def space_peer(d):
        return lax.rem(s0 + d, n_space)

    def yaw_peer(d):
        return lax.rem(y0 + d, n_yaw)

    has_before, has_after = s0 > 0, s0 < n_space - 1
    last = jnp.logical_not(has_after)

    barrier = pltpu.get_barrier_semaphore()

    def enter(slab):
        pl.semaphore_signal(barrier, inc=1, device_id={"space": slab})

    pl.when(has_before)(lambda: enter(s0 - 1))
    pl.when(has_after)(lambda: enter(s0 + 1))
    loads = [
        pltpu.make_async_copy(src, dst, load.at[i])
        for i, (src, dst) in enumerate((
            (adj_in, adj), (visc_in, visc), (coup_in, coup), (cell_in, cell), (patch_in, patch),
            (normal_in, normal), (weight_in, weight), (tile_in, tile),
        ))
    ]
    for copy in loads[:2]:
        copy.start()
    each(n_space - 1, lambda slab: pl.when(slab > s0 + 1)(lambda: enter(slab)), 2)
    for copy in loads[2:]:
        copy.start()
    grads[...] = jnp.zeros_like(grads)

    core = lax.rem(s0, 2)
    first = s0 - core
    turn = lax.rem(y0, 2)
    mine = first + turn
    is_site = core == 1
    own_morph = pltpu.make_async_copy(morph_in, morph, load.at[8])
    near_morph = pltpu.make_async_remote_copy(
        src_ref=morph_in, dst_ref=morph, send_sem=morph_send, recv_sem=morph_recv,
        device_id={"space": first + 1},
    )
    uses_own = jnp.logical_and(is_site, turn == 1)
    gets_near = jnp.logical_and(is_site, turn == 0)
    gives_near = jnp.logical_and(core == 0, turn == 0)

    @pl.when(uses_own)
    def _():
        own_morph.start()

    @pl.when(has_after)
    def _():
        pl.semaphore_wait(barrier, s0 + 1)

    @pl.when(s0 == n_space - 2)
    def _():
        pl.semaphore_signal(row_in, inc=1, device_id={"space": n_space - 1})

    @pl.when(last)
    def _():
        pl.semaphore_wait(row_in, 1)
        each(n_yaw, lambda d: pl.semaphore_signal(barrier, inc=1, device_id={"yaw": yaw_peer(d)}))
        pl.semaphore_wait(barrier, n_yaw)
        each(n_space - 1, lambda slab: pl.semaphore_signal(all_in, inc=1, device_id={"space": slab}), 0)

    def halo(slot, src, dst, peer):
        return pltpu.make_async_remote_copy(
            src_ref=src, dst_ref=dst, send_sem=halo_send.at[slot], recv_sem=halo_recv.at[slot],
            device_id={"space": peer},
        )

    up = (
        halo(0, adj.at[0, :, layers - 1], before_a, s0 + 1),
        halo(1, visc.at[0, layers - 1], before_v, s0 + 1),
    )
    down = (
        halo(2, adj_in.at[0, :, 0], after_a, s0 - 1),
        halo(3, visc_in.at[0, 0], after_v, s0 - 1),
    )

    @pl.when(jnp.logical_and(has_before, core == 0))
    def _():
        for copy in down:
            copy.start()

    for copy in loads[:2]:
        copy.wait()

    @pl.when(has_after)
    def _():
        for copy in up:
            copy.start()

    @pl.when(core == 1)
    def _():
        for copy in down:
            copy.start()

    @pl.when(gives_near)
    def _():
        near_morph.start()

    @pl.when(jnp.logical_not(has_before))
    def _():
        before_a[...] = jnp.zeros_like(before_a)
        before_v[...] = jnp.zeros_like(before_v)

    @pl.when(jnp.logical_not(has_after))
    def _():
        after_a[...] = jnp.zeros_like(after_a)
        after_v[...] = jnp.zeros_like(after_v)

    for copy in loads[2:]:
        copy.wait()

    at_y = lax.broadcasted_iota(jnp.int32, (ny, nz), 0)
    at_z = lax.broadcasted_iota(jnp.int32, (ny, nz), 1)
    shifts = (
        (0, 1, at_y > 0), (0, ny - 1, at_y < ny - 1), (1, 1, at_z > 0), (1, nz - 1, at_z < nz - 1)
    )
    for x in range(layers):
        v = visc[0, x]
        total = jnp.zeros_like(v)
        faces = []
        for axis, shift, inside in shifts:
            face = 0.5 * (v + jnp.where(inside, pltpu.roll(v, shift, axis), 0.0))
            total = total + face
            faces.append(jnp.where(inside, face, 0.0))
        inner = {}
        for nb in (x - 1, x + 1):
            if 0 <= nb < layers:
                inner[nb] = 0.5 * (v + visc[0, nb])
                total = total + inner[nb]
        total = total + 2.0
        acc = jnp.zeros_like(v)
        for f in range(fields):
            a = adj[0, f, x]
            out = total * a
            for g in range(fields):
                out = out + coup[0, f, g] * adj[0, g, x]
            for (axis, shift, _), face in zip(shifts, faces):
                out = out - face * pltpu.roll(a, shift, axis)
            for nb, face in inner.items():
                out = out - face * adj[0, f, nb]
            res[0, f, x] = out
            acc = acc + a * out
        inner_sens[x] = acc

    cells = layers * ny
    for j in range(nodes // CHUNK):
        at = pl.ds(j * CHUNK, CHUNK)
        c = cell[:, at]
        row = (c // LANES) % groups * cells + c // nz
        count = groups * cells
        hot = (lax.broadcasted_iota(jnp.int32, (count, CHUNK), 0) == row).astype(F32).astype(BF16)
        pick_row[0:count, at] = hot
        pick_row[count:2 * count, at] = hot
        low = patch[:, at] % LANES
        hot = (lax.broadcasted_iota(jnp.int32, (LANES, CHUNK), 0) == low).astype(F32)
        pick_patch_t[at, :] = hot.T.astype(BF16)
    normal8[...] = jnp.zeros_like(normal8)
    for h in range(halves):
        normal8[3 * h:3 * h + 3, :] = normal[...]

    @pl.when(uses_own)
    def _():
        own_morph.wait()

    @pl.when(gets_near)
    def _():
        near_morph.wait_recv()

    @pl.when(is_site)
    def _():
        m_hi, m_lo = parts(morph[...].T)
        morph_hi[...] = m_hi
        morph_lo[...] = m_lo

    @pl.when(has_before)
    def _():
        for copy in up:
            copy.wait_recv()

    @pl.when(has_after)
    def _():
        for copy in down:
            copy.wait_recv()

    def outer(x):
        return [(before_a, before_v)] * (x == 0) + [(after_a, after_v)] * (x == layers - 1)

    cell_sens = []
    for x in range(layers):
        v = visc[0, x]
        acc = inner_sens[x]
        for far_a, far_v in outer(x):
            across = jnp.zeros_like(v)
            for f in range(fields):
                a = adj[0, f, x]
                across = across + a * (far_a[f] - a)
            acc = acc - 0.5 * (v + far_v[...]) * across
        cell_sens.append(weight[0] * v * acc)
    s = jnp.concatenate(cell_sens, axis=0)
    s = jnp.concatenate([s[:, g * LANES:(g + 1) * LANES] for g in range(groups)], axis=0)
    s = jnp.concatenate(parts(s.T), axis=1)

    owner_rows = n_space * rows
    wide = WIDE if nodes % WIDE == 0 else CHUNK
    shape3 = (n_space, rows, wide)
    half_of = lax.broadcasted_iota(jnp.int32, shape3, 0) * halves + lax.broadcasted_iota(jnp.int32, shape3, 1) // 3
    sums_now = jnp.zeros((2 * owner_rows, LANES), F32)
    for j in range(nodes // wide):
        at = pl.ds(j * wide, wide)
        t = dot(s, pick_row[:, at])
        lane = cell[:, at] % LANES
        here = lax.broadcasted_iota(jnp.int32, t.shape, 0) == lane
        sens = jnp.sum(jnp.where(here, t, 0.0), axis=0, keepdims=True)
        part = normal8[:, at] * sens
        hi = part.astype(BF16).astype(F32)
        chosen = half_of == (patch[:, at] // LANES)[None]
        a = jnp.concatenate([
            jnp.where(chosen, piece[None], 0.0).reshape(owner_rows, wide).astype(BF16) for piece in (hi, part - hi)
        ], axis=0)
        sums_now = sums_now + dot(a, pick_patch_t[at, :])
    dense[...] = (sums_now[:owner_rows] + sums_now[owner_rows:]).reshape(dense.shape)

    pair = lax.div(y0, 2)

    def slot(yaw, slab):
        return lax.rem(y0 - yaw + n_yaw, n_yaw) * n_space + lax.rem(s0 - slab + n_space, n_space)

    def wait_blocks(sem, start, count):
        blocks = got.at[start:start + count, 0:used]
        pltpu.make_async_copy(blocks, blocks, sem).wait()

    def to_site(q, owner):
        odd = lax.rem(owner, 2)
        return pltpu.make_async_remote_copy(
            src_ref=dense.at[owner, 0:used],
            dst_ref=got.at[slot(2 * q + odd, owner - odd + 1), 0:used],
            send_sem=send1, recv_sem=recv1,
            device_id={"yaw": 2 * q + odd, "space": owner - odd + 1},
        )

    pl.when(has_after)(lambda: pl.semaphore_wait(all_in, 1))
    def to_sites(q, i):
        owner = n_space - 1 - i

        @pl.when(jnp.logical_not(jnp.logical_and(is_site, jnp.logical_and(pair == q, owner == mine))))
        def _():
            to_site(q, owner).start()

    for q in range(n_yaw // 2):
        each(n_space, functools.partial(to_sites, q), 0)

    for x in range(layers):
        v = visc[0, x]
        for far_a, far_v in outer(x):
            face = 0.5 * (v + far_v[...])
            for f in range(fields):
                res[0, f, x] = res[0, f, x] - face * (far_a[f] - adj[0, f, x])

    def to_slab(k, slab):
        return pltpu.make_async_remote_copy(
            src_ref=grads.at[mine, 0:used], dst_ref=grads.at[mine, 0:used],
            send_sem=send3, recv_sem=recv3,
            device_id={"yaw": 2 * pair + k, "space": slab},
        )

    def to_slabs(slab):
        for k in range(2):
            @pl.when(jnp.logical_not(jnp.logical_and(slab == s0, turn == k)))
            def _():
                to_slab(k, slab).start()

    @pl.when(is_site)
    def _():
        got[0] = dense[mine]
        wait_blocks(recv1, 1, n_yaw * n_space - 1)
        p = jnp.sum(got[...], axis=0)
        p = jnp.concatenate([p[3 * h:3 * h + 3] for h in range(halves)], axis=1)
        p = jnp.concatenate([p, jnp.zeros((5, owned), F32)], axis=0)
        hi, lo = parts(p)
        both = jnp.concatenate([hi.astype(F32), lo.astype(F32)], axis=0).astype(BF16)
        smooth = dot(both, morph_hi[...]) + dot(both, morph_lo[...])
        g = p + smooth[0:8] + smooth[8:16]
        for h in range(halves):
            grads[mine, 3 * h:3 * h + 3] = g[0:3, h * LANES:(h + 1) * LANES]
        each(n_space, to_slabs, 0)

    @pl.when(has_before)
    def _():
        for copy in down:
            copy.wait_send()

    @pl.when(has_after)
    def _():
        for copy in up:
            copy.wait_send()

    @pl.when(gives_near)
    def _():
        near_morph.wait_send()

    sent = n_yaw // 2 * n_space

    @pl.when(is_site)
    def _():
        wait_blocks(send1, 0, sent - 1)
        wait_blocks(recv3, 0, n_space - 1)

    @pl.when(jnp.logical_not(is_site))
    def _():
        wait_blocks(send1, 0, sent)
        wait_blocks(recv3, 0, n_space)

    for h in range(halves):
        pgrad[:, h * LANES:(h + 1) * LANES] = grads[s0, 3 * h:3 * h + 3]
    grads_out[...] = grads[...]

    @pl.when(is_site)
    def _():
        wait_blocks(send3, 0, 2 * n_space - 1)


def finish(res, pgrad, grads, tile, res_out, pgrad_out, ngrad_out, ngrad, sem):
    n_space = grads.shape[0]
    halves = pgrad.shape[1] // LANES
    copies = [
        pltpu.make_async_copy(src, dst, sem.at[i])
        for i, (src, dst) in enumerate(((res, res_out), (pgrad, pgrad_out), (ngrad, ngrad_out)))
    ]
    for copy in copies[:2]:
        copy.start()
    for block in range(tile.shape[0] // 8):
        node_patch = tile[8 * block:8 * block + 8]
        low, high = node_patch % LANES, node_patch // LANES
        out = [jnp.zeros(low.shape, F32)] * 3
        for owner in range(n_space):
            for h in range(halves):
                here = high == owner * halves + h
                for c in range(3):
                    row = jnp.broadcast_to(grads[owner, 3 * h + c:3 * h + c + 1], low.shape)
                    value = jnp.take_along_axis(row, low, axis=1, mode="promise_in_bounds")
                    out[c] = jnp.where(here, value, out[c])
        for c in range(3):
            for r in range(8):
                at = (8 * block + r) * LANES
                ngrad[c:c + 1, at:at + LANES] = out[c][r:r + 1]
    copies[2].start()
    for copy in copies:
        copy.wait()


def shards(
    n_yaw, n_space,
    adjoint, viscosity, coupling, yaw_weight, node_cell, node_patch, node_normal, morph_kernel,
):
    _, fields, layers, ny, nz = adjoint.shape
    nodes = node_cell.shape[0]
    owned = morph_kernel.shape[1]
    rows = -(-3 * (owned // LANES) // 8) * 8
    vmem = pl.BlockSpec(memory_space=pltpu.VMEM)
    anywhere = pl.BlockSpec(memory_space=pl.ANY)
    dma = pltpu.SemaphoreType.DMA
    outs = pl.pallas_call(
        functools.partial(kernel, n_yaw, n_space),
        out_shape=(
            pltpu.VMEM(adjoint.shape, F32),
            pltpu.VMEM((3, owned), F32),
            pltpu.VMEM((n_space, rows, LANES), F32),
            pltpu.VMEM((nodes // LANES, LANES), jnp.int32),
        ),
        in_specs=[pl.BlockSpec(memory_space=pltpu.HBM)] * 9,
        out_specs=(vmem,) * 4,
        scratch_shapes=[
            pltpu.SMEM(coupling.shape, F32),
            pltpu.SMEM((1,), F32),
            pltpu.VMEM(adjoint.shape, F32),
            pltpu.VMEM(viscosity.shape, F32),
            pltpu.VMEM((1, nodes), jnp.int32),
            pltpu.VMEM((1, nodes), jnp.int32),
            pltpu.VMEM(node_normal.shape, F32),
            pltpu.VMEM(morph_kernel.shape, F32),
            pltpu.VMEM((fields, ny, nz), F32),
            pltpu.VMEM((ny, nz), F32),
            pltpu.VMEM((fields, ny, nz), F32),
            pltpu.VMEM((ny, nz), F32),
            pltpu.VMEM((2 * layers * ny * nz // LANES, nodes), BF16),
            pltpu.VMEM((nodes, LANES), BF16),
            pltpu.VMEM((rows, nodes), F32),
            pltpu.VMEM((owned, owned), BF16),
            pltpu.VMEM((owned, owned), BF16),
            pltpu.VMEM((layers, ny, nz), F32),
            pltpu.VMEM((n_space, rows, LANES), F32),
            pltpu.VMEM((n_yaw * n_space, rows, LANES), F32),
            pltpu.VMEM((n_space, rows, LANES), F32),
            pltpu.SemaphoreType.REGULAR, pltpu.SemaphoreType.REGULAR,
            dma((9,)), dma((4,)), dma((4,)),
            dma, dma, dma, dma, dma, dma,
        ],
        compiler_params=pltpu.CompilerParams(
            collective_id=0, has_side_effects=True, vmem_limit_bytes=56 * 1024 * 1024
        ),
        cost_estimate=pl.CostEstimate(flops=400_000_000, bytes_accessed=1_000_000, transcendentals=0),
    )(
        coupling, yaw_weight, adjoint, viscosity,
        node_cell[None], node_patch[None], node_patch.reshape(nodes // LANES, LANES), node_normal, morph_kernel,
    )
    return pl.pallas_call(
        finish,
        out_shape=(
            jax.ShapeDtypeStruct(adjoint.shape, F32),
            jax.ShapeDtypeStruct((3, owned), F32),
            jax.ShapeDtypeStruct((3, nodes), F32),
        ),
        in_specs=[vmem] * 4,
        out_specs=(anywhere,) * 3,
        scratch_shapes=[pltpu.VMEM((3, nodes), F32), dma((3,))],
        compiler_params=pltpu.CompilerParams(vmem_limit_bytes=4 * 1024 * 1024),
    )(*outs)


def solution(mesh):
    return jax.shard_map(
        functools.partial(shards, mesh.shape["yaw"], mesh.shape["space"]),
        mesh=mesh,
        in_specs=(
            P("yaw", None, "space", None, None),
            P("yaw", "space", None, None),
            P("yaw", None, None),
            P("yaw"),
            P("space"),
            P("space"),
            P(None, "space"),
            P("space", None),
        ),
        out_specs=(P("yaw", None, "space", None, None), P(None, "space"), P(None, "space")),
        check_vma=False,
    )
```

```python
import functools

import jax
import jax.numpy as jnp
from jax import lax
from jax.experimental import pallas as pl
from jax.experimental.pallas import tpu as pltpu
from jax.sharding import PartitionSpec as P

LANES = 128
CHUNK = 256
F32 = jnp.float32
BF16 = jnp.bfloat16


def dot(a, b, contract=((1,), (0,))):
    return lax.dot_general(a, b, (contract, ((), ())), preferred_element_type=F32)


def parts(x):
    hi = x.astype(BF16)
    return hi, (x - hi.astype(F32)).astype(BF16)


def each(count, body, first=1):
    if count <= 8:
        for d in range(first, count):
            body(d)
    else:
        lax.fori_loop(first, count, lambda d, c: (body(d), c)[1], 0)


def kernel(
    n_yaw, n_space,
    coup_in, weight_in, adj_in, visc_in, cell_in, patch_in, tile_in, normal_in, morph_in,
    res, pgrad, grads_out, tile,
    coup, weight, adj, visc, cell, patch, normal, morph,
    far_a, far_v,
    cell_sens, near_sens, pick_patch_t, normal8, morph_hi, morph_lo,
    inner_sens, dense, got, grads,
    row_in, all_in, load, halo_send, halo_recv, send1, recv1, send3, recv3, morph_send, morph_recv,
):
    _, fields, layers, ny, nz = adj.shape
    nodes = patch.shape[1]
    owned = morph.shape[1]
    halves = owned // LANES
    used = 3 * halves
    rows = dense.shape[1]
    groups = nz // LANES
    y0, s0 = lax.axis_index("yaw"), lax.axis_index("space")

    def space_peer(d):
        return lax.rem(s0 + d, n_space)

    def yaw_peer(d):
        return lax.rem(y0 + d, n_yaw)

    has_before, has_after = s0 > 0, s0 < n_space - 1
    last = jnp.logical_not(has_after)

    barrier = pltpu.get_barrier_semaphore()

    def enter(slab):
        pl.semaphore_signal(barrier, inc=1, device_id={"space": slab})

    pl.when(has_before)(lambda: enter(s0 - 1))
    pl.when(has_after)(lambda: enter(s0 + 1))
    loads = [
        pltpu.make_async_copy(src, dst, load.at[i])
        for i, (src, dst) in enumerate((
            (adj_in, adj), (visc_in, visc), (coup_in, coup), (cell_in, cell), (patch_in, patch),
            (normal_in, normal), (weight_in, weight), (tile_in, tile),
        ))
    ]
    for copy in loads[:2]:
        copy.start()
    each(n_space - 1, lambda slab: pl.when(slab > s0 + 1)(lambda: enter(slab)), 2)
    for copy in loads[2:]:
        copy.start()
    grads[...] = jnp.zeros_like(grads)

    core = lax.rem(s0, 2)
    first = s0 - core
    turn = lax.rem(y0, 2)
    mine = first + turn
    is_site = core == 1
    own_morph = pltpu.make_async_copy(morph_in, morph, load.at[8])
    near_morph = pltpu.make_async_remote_copy(
        src_ref=morph_in, dst_ref=morph, send_sem=morph_send, recv_sem=morph_recv,
        device_id={"space": first + 1},
    )
    uses_own = jnp.logical_and(is_site, turn == 1)
    gets_near = jnp.logical_and(is_site, turn == 0)
    gives_near = jnp.logical_and(core == 0, turn == 0)

    @pl.when(uses_own)
    def _():
        own_morph.start()

    @pl.when(has_after)
    def _():
        pl.semaphore_wait(barrier, s0 + 1)

    @pl.when(s0 == n_space - 2)
    def _():
        pl.semaphore_signal(row_in, inc=1, device_id={"space": n_space - 1})

    @pl.when(last)
    def _():
        pl.semaphore_wait(row_in, 1)
        each(n_yaw, lambda d: pl.semaphore_signal(barrier, inc=1, device_id={"yaw": yaw_peer(d)}))
        pl.semaphore_wait(barrier, n_yaw)
        each(n_space - 1, lambda slab: pl.semaphore_signal(all_in, inc=1, device_id={"space": slab}), 0)

    def halo(slot, src, dst, peer):
        return pltpu.make_async_remote_copy(
            src_ref=src, dst_ref=dst, send_sem=halo_send.at[slot], recv_sem=halo_recv.at[slot],
            device_id={"space": peer},
        )

    up = (
        halo(0, adj.at[0, :, layers - 1], far_a.at[0], s0 + 1),
        halo(1, visc.at[0, layers - 1], far_v.at[0], s0 + 1),
    )
    down = (
        halo(2, adj_in.at[0, :, 0], far_a.at[1], s0 - 1),
        halo(3, visc_in.at[0, 0], far_v.at[1], s0 - 1),
    )

    @pl.when(jnp.logical_and(has_before, core == 0))
    def _():
        for copy in down:
            copy.start()

    for copy in loads[:2]:
        copy.wait()

    @pl.when(has_after)
    def _():
        for copy in up:
            copy.start()

    @pl.when(core == 1)
    def _():
        for copy in down:
            copy.start()

    @pl.when(gives_near)
    def _():
        near_morph.start()

    @pl.when(jnp.logical_not(has_before))
    def _():
        far_a[0] = jnp.zeros_like(far_a[0])
        far_v[0] = jnp.zeros_like(far_v[0])

    @pl.when(jnp.logical_not(has_after))
    def _():
        far_a[1] = jnp.zeros_like(far_a[1])
        far_v[1] = jnp.zeros_like(far_v[1])

    for copy in loads[2:]:
        copy.wait()

    at_y = lax.broadcasted_iota(jnp.int32, (ny, nz), 0)
    at_z = lax.broadcasted_iota(jnp.int32, (ny, nz), 1)
    shifts = (
        (0, 1, at_y > 0), (0, ny - 1, at_y < ny - 1), (1, 1, at_z > 0), (1, nz - 1, at_z < nz - 1)
    )
    for x in range(layers):
        v = visc[0, x]
        total = jnp.zeros_like(v)
        faces = []
        for axis, shift, inside in shifts:
            face = 0.5 * (v + jnp.where(inside, pltpu.roll(v, shift, axis), 0.0))
            total = total + face
            faces.append(jnp.where(inside, face, 0.0))
        inner = {}
        for nb in (x - 1, x + 1):
            if 0 <= nb < layers:
                inner[nb] = 0.5 * (v + visc[0, nb])
                total = total + inner[nb]
        total = total + 2.0
        acc = jnp.zeros_like(v)
        for f in range(fields):
            a = adj[0, f, x]
            out = total * a
            for g in range(fields):
                out = out + coup[0, f, g] * adj[0, g, x]
            for (axis, shift, _), face in zip(shifts, faces):
                out = out - face * pltpu.roll(a, shift, axis)
            for nb, face in inner.items():
                out = out - face * adj[0, f, nb]
            res[0, f, x] = out
            acc = acc + a * out
        inner_sens[x] = acc

    for j in range(nodes // CHUNK):
        at = pl.ds(j * CHUNK, CHUNK)
        low = patch[:, at] % LANES
        hot = (lax.broadcasted_iota(jnp.int32, (LANES, CHUNK), 0) == low).astype(F32)
        pick_patch_t[at, :] = hot.T.astype(BF16)
    normal8[...] = jnp.zeros_like(normal8)
    for h in range(halves):
        normal8[3 * h:3 * h + 3, :] = normal[...]

    @pl.when(uses_own)
    def _():
        own_morph.wait()

    @pl.when(gets_near)
    def _():
        near_morph.wait_recv()

    @pl.when(is_site)
    def _():
        m_hi, m_lo = parts(morph[...].T)
        morph_hi[...] = m_hi
        morph_lo[...] = m_lo

    def sens_of(side):
        x = side * (layers - 1)
        v = visc[0, x]
        across = jnp.zeros_like(v)
        for f in range(fields):
            a = adj[0, f, x]
            across = across + a * (far_a[side, f] - a)
        acc = inner_sens[x] - 0.5 * (v + far_v[side]) * across
        cell_sens[side] = weight[0] * v * acc

    def at_nodes(side, block):
        here = cell[8 * block:8 * block + 8]
        lane, row = here % LANES, here // LANES - side * ((layers - 1) * ny * groups)
        found = [jnp.zeros(lane.shape, F32)] * groups
        for y in range(ny):
            for g in range(groups):
                source = jnp.broadcast_to(cell_sens[side, y:y + 1, g * LANES:(g + 1) * LANES], lane.shape)
                value = jnp.take_along_axis(source, lane, axis=1, mode="promise_in_bounds")
                found[g] = jnp.where(row == y * groups + g, value, found[g])
        return sum(found[1:], found[0])

    @pl.when(jnp.logical_and(core == 0, has_after))
    def _():
        for copy in down:
            copy.wait_recv()

    @pl.when(core == 1)
    def _():
        for copy in up:
            copy.wait_recv()

    sens_of(1 - core)
    for block in range(nodes // (8 * LANES)):
        near_sens[8 * block:8 * block + 8] = at_nodes(1 - core, block)

    @pl.when(jnp.logical_and(core == 0, has_before))
    def _():
        for copy in up:
            copy.wait_recv()

    @pl.when(jnp.logical_and(core == 1, has_after))
    def _():
        for copy in down:
            copy.wait_recv()

    sens_of(core)
    owner_rows = n_space * rows
    wide = 8 * LANES
    shape3 = (n_space, rows, wide)
    half_of = lax.broadcasted_iota(jnp.int32, shape3, 0) * halves + lax.broadcasted_iota(jnp.int32, shape3, 1) // 3
    sums_now = jnp.zeros((2 * owner_rows, LANES), F32)
    for j in range(nodes // wide):
        at = pl.ds(j * wide, wide)
        sens = near_sens[8 * j:8 * j + 8] + at_nodes(core, j)
        part = jnp.concatenate([
            normal8[:, j * wide + r * LANES:j * wide + (r + 1) * LANES] * sens[r:r + 1] for r in range(8)
        ], axis=1)
        hi = part.astype(BF16).astype(F32)
        chosen = half_of == (patch[:, at] // LANES)[None]
        a = jnp.concatenate([
            jnp.where(chosen, piece[None], 0.0).reshape(owner_rows, wide).astype(BF16) for piece in (hi, part - hi)
        ], axis=0)
        sums_now = sums_now + dot(a, pick_patch_t[at, :])
    dense[...] = (sums_now[:owner_rows] + sums_now[owner_rows:]).reshape(dense.shape)

    pair = lax.div(y0, 2)

    def slot(yaw, slab):
        return lax.rem(y0 - yaw + n_yaw, n_yaw) * n_space + lax.rem(s0 - slab + n_space, n_space)

    def wait_blocks(sem, start, count):
        blocks = got.at[start:start + count, 0:used]
        pltpu.make_async_copy(blocks, blocks, sem).wait()

    def to_site(q, owner):
        odd = lax.rem(owner, 2)
        return pltpu.make_async_remote_copy(
            src_ref=dense.at[owner, 0:used],
            dst_ref=got.at[slot(2 * q + odd, owner - odd + 1), 0:used],
            send_sem=send1, recv_sem=recv1,
            device_id={"yaw": 2 * q + odd, "space": owner - odd + 1},
        )

    pl.when(has_after)(lambda: pl.semaphore_wait(all_in, 1))
    def to_sites(q, i):
        owner = n_space - 1 - i

        @pl.when(jnp.logical_not(jnp.logical_and(is_site, jnp.logical_and(pair == q, owner == mine))))
        def _():
            to_site(q, owner).start()

    for q in range(n_yaw // 2):
        each(n_space, functools.partial(to_sites, q), 0)

    for side in range(2):
        x = side * (layers - 1)
        face = 0.5 * (visc[0, x] + far_v[side])
        for f in range(fields):
            res[0, f, x] = res[0, f, x] - face * (far_a[side, f] - adj[0, f, x])

    def to_slab(k, slab):
        return pltpu.make_async_remote_copy(
            src_ref=grads.at[mine, 0:used], dst_ref=grads.at[mine, 0:used],
            send_sem=send3, recv_sem=recv3,
            device_id={"yaw": 2 * pair + k, "space": slab},
        )

    def to_slabs(slab):
        for k in range(2):
            @pl.when(jnp.logical_not(jnp.logical_and(slab == s0, turn == k)))
            def _():
                to_slab(k, slab).start()

    @pl.when(is_site)
    def _():
        got[0] = dense[mine]
        wait_blocks(recv1, 1, n_yaw * n_space - 1)
        p = jnp.sum(got[...], axis=0)
        p = jnp.concatenate([p[3 * h:3 * h + 3] for h in range(halves)], axis=1)
        p = jnp.concatenate([p, jnp.zeros((5, owned), F32)], axis=0)
        hi, lo = parts(p)
        both = jnp.concatenate([hi.astype(F32), lo.astype(F32)], axis=0).astype(BF16)
        smooth = dot(both, morph_hi[...]) + dot(both, morph_lo[...])
        g = p + smooth[0:8] + smooth[8:16]
        for h in range(halves):
            grads[mine, 3 * h:3 * h + 3] = g[0:3, h * LANES:(h + 1) * LANES]
        each(n_space, to_slabs, 0)

    @pl.when(has_before)
    def _():
        for copy in down:
            copy.wait_send()

    @pl.when(has_after)
    def _():
        for copy in up:
            copy.wait_send()

    @pl.when(gives_near)
    def _():
        near_morph.wait_send()

    sent = n_yaw // 2 * n_space

    @pl.when(is_site)
    def _():
        wait_blocks(send1, 0, sent - 1)
        wait_blocks(recv3, 0, n_space - 1)

    @pl.when(jnp.logical_not(is_site))
    def _():
        wait_blocks(send1, 0, sent)
        wait_blocks(recv3, 0, n_space)

    for h in range(halves):
        pgrad[:, h * LANES:(h + 1) * LANES] = grads[s0, 3 * h:3 * h + 3]
    grads_out[...] = grads[...]

    @pl.when(is_site)
    def _():
        wait_blocks(send3, 0, 2 * n_space - 1)


def finish(res, pgrad, grads, tile, res_out, pgrad_out, ngrad_out, ngrad, sem):
    n_space = grads.shape[0]
    halves = pgrad.shape[1] // LANES
    copies = [
        pltpu.make_async_copy(src, dst, sem.at[i])
        for i, (src, dst) in enumerate(((res, res_out), (pgrad, pgrad_out), (ngrad, ngrad_out)))
    ]
    for copy in copies[:2]:
        copy.start()
    for block in range(tile.shape[0] // 8):
        node_patch = tile[8 * block:8 * block + 8]
        low, high = node_patch % LANES, node_patch // LANES
        out = [jnp.zeros(low.shape, F32)] * 3
        for owner in range(n_space):
            for h in range(halves):
                here = high == owner * halves + h
                for c in range(3):
                    row = jnp.broadcast_to(grads[owner, 3 * h + c:3 * h + c + 1], low.shape)
                    value = jnp.take_along_axis(row, low, axis=1, mode="promise_in_bounds")
                    out[c] = jnp.where(here, value, out[c])
        for c in range(3):
            for r in range(8):
                at = (8 * block + r) * LANES
                ngrad[c:c + 1, at:at + LANES] = out[c][r:r + 1]
    copies[2].start()
    for copy in copies:
        copy.wait()


def shards(
    n_yaw, n_space,
    adjoint, viscosity, coupling, yaw_weight, node_cell, node_patch, node_normal, morph_kernel,
):
    _, fields, layers, ny, nz = adjoint.shape
    nodes = node_cell.shape[0]
    owned = morph_kernel.shape[1]
    rows = -(-3 * (owned // LANES) // 8) * 8
    vmem = pl.BlockSpec(memory_space=pltpu.VMEM)
    anywhere = pl.BlockSpec(memory_space=pl.ANY)
    dma = pltpu.SemaphoreType.DMA
    outs = pl.pallas_call(
        functools.partial(kernel, n_yaw, n_space),
        out_shape=(
            pltpu.VMEM(adjoint.shape, F32),
            pltpu.VMEM((3, owned), F32),
            pltpu.VMEM((n_space, rows, LANES), F32),
            pltpu.VMEM((nodes // LANES, LANES), jnp.int32),
        ),
        in_specs=[pl.BlockSpec(memory_space=pltpu.HBM)] * 9,
        out_specs=(vmem,) * 4,
        scratch_shapes=[
            pltpu.SMEM(coupling.shape, F32),
            pltpu.SMEM((1,), F32),
            pltpu.VMEM(adjoint.shape, F32),
            pltpu.VMEM(viscosity.shape, F32),
            pltpu.VMEM((nodes // LANES, LANES), jnp.int32),
            pltpu.VMEM((1, nodes), jnp.int32),
            pltpu.VMEM(node_normal.shape, F32),
            pltpu.VMEM(morph_kernel.shape, F32),
            pltpu.VMEM((2, fields, ny, nz), F32),
            pltpu.VMEM((2, ny, nz), F32),
            pltpu.VMEM((2, ny, nz), F32),
            pltpu.VMEM((nodes // LANES, LANES), F32),
            pltpu.VMEM((nodes, LANES), BF16),
            pltpu.VMEM((rows, nodes), F32),
            pltpu.VMEM((owned, owned), BF16),
            pltpu.VMEM((owned, owned), BF16),
            pltpu.VMEM((layers, ny, nz), F32),
            pltpu.VMEM((n_space, rows, LANES), F32),
            pltpu.VMEM((n_yaw * n_space, rows, LANES), F32),
            pltpu.VMEM((n_space, rows, LANES), F32),
            pltpu.SemaphoreType.REGULAR, pltpu.SemaphoreType.REGULAR,
            dma((9,)), dma((4,)), dma((4,)),
            dma, dma, dma, dma, dma, dma,
        ],
        compiler_params=pltpu.CompilerParams(
            collective_id=0, has_side_effects=True, vmem_limit_bytes=56 * 1024 * 1024
        ),
        cost_estimate=pl.CostEstimate(flops=400_000_000, bytes_accessed=1_000_000, transcendentals=0),
    )(
        coupling, yaw_weight, adjoint, viscosity,
        node_cell.reshape(nodes // LANES, LANES), node_patch[None], node_patch.reshape(nodes // LANES, LANES), node_normal, morph_kernel,
    )
    return pl.pallas_call(
        finish,
        out_shape=(
            jax.ShapeDtypeStruct(adjoint.shape, F32),
            jax.ShapeDtypeStruct((3, owned), F32),
            jax.ShapeDtypeStruct((3, nodes), F32),
        ),
        in_specs=[vmem] * 4,
        out_specs=(anywhere,) * 3,
        scratch_shapes=[pltpu.VMEM((3, nodes), F32), dma((3,))],
        compiler_params=pltpu.CompilerParams(vmem_limit_bytes=4 * 1024 * 1024),
    )(*outs)


def solution(mesh):
    return jax.shard_map(
        functools.partial(shards, mesh.shape["yaw"], mesh.shape["space"]),
        mesh=mesh,
        in_specs=(
            P("yaw", None, "space", None, None),
            P("yaw", "space", None, None),
            P("yaw", None, None),
            P("yaw"),
            P("space"),
            P("space"),
            P(None, "space"),
            P("space", None),
        ),
        out_specs=(P("yaw", None, "space", None, None), P(None, "space"), P(None, "space")),
        check_vma=False,
    )
```

```python
import functools

import jax
import jax.numpy as jnp
from jax import lax
from jax.experimental import pallas as pl
from jax.experimental.pallas import tpu as pltpu
from jax.sharding import PartitionSpec as P

LANES = 128
CHUNK = 256
F32 = jnp.float32
BF16 = jnp.bfloat16


def dot(a, b, contract=((1,), (0,))):
    return lax.dot_general(a, b, (contract, ((), ())), preferred_element_type=F32)


def parts(x):
    hi = x.astype(BF16)
    return hi, (x - hi.astype(F32)).astype(BF16)


def each(count, body, first=1):
    if count <= 8:
        for d in range(first, count):
            body(d)
    else:
        lax.fori_loop(first, count, lambda d, c: (body(d), c)[1], 0)


def kernel(
    n_yaw, n_space,
    coup_in, weight_in, adj_in, visc_in, cell_in, patch_in, tile_in, normal_in, morph_in,
    res, pgrad, grads_out, tile,
    coup, weight, adj, visc, cell, patch, normal, morph,
    far_a, far_v,
    cell_sens, near_sens, pick_patch_t, normal8, morph_hi, morph_lo,
    inner_sens, dense, got, grads,
    row_in, all_in, load, halo_send, halo_recv, send1, recv1, send3, recv3, morph_send, morph_recv,
):
    _, fields, layers, ny, nz = adj.shape
    nodes = patch.shape[1]
    owned = morph.shape[1]
    halves = owned // LANES
    used = 3 * halves
    rows = dense.shape[1]
    groups = nz // LANES
    y0, s0 = lax.axis_index("yaw"), lax.axis_index("space")

    def space_peer(d):
        return lax.rem(s0 + d, n_space)

    def yaw_peer(d):
        return lax.rem(y0 + d, n_yaw)

    has_before, has_after = s0 > 0, s0 < n_space - 1
    last = jnp.logical_not(has_after)

    barrier = pltpu.get_barrier_semaphore()

    def enter(slab):
        pl.semaphore_signal(barrier, inc=1, device_id={"space": slab})

    pl.when(has_before)(lambda: enter(s0 - 1))
    pl.when(has_after)(lambda: enter(s0 + 1))
    loads = [
        pltpu.make_async_copy(src, dst, load.at[i])
        for i, (src, dst) in enumerate((
            (adj_in, adj), (visc_in, visc), (coup_in, coup), (cell_in, cell), (patch_in, patch),
            (normal_in, normal), (weight_in, weight), (tile_in, tile),
        ))
    ]
    for copy in loads[:2]:
        copy.start()
    each(n_space - 1, lambda slab: pl.when(slab > s0 + 1)(lambda: enter(slab)), 2)
    grads[...] = jnp.zeros_like(grads)

    core = lax.rem(s0, 2)
    first = s0 - core
    turn = lax.rem(y0, 2)
    mine = first + turn
    is_site = core == 1
    own_morph = pltpu.make_async_copy(morph_in, morph, load.at[8])
    near_morph = pltpu.make_async_remote_copy(
        src_ref=morph_in, dst_ref=morph, send_sem=morph_send, recv_sem=morph_recv,
        device_id={"space": first + 1},
    )
    uses_own = jnp.logical_and(is_site, turn == 1)
    gets_near = jnp.logical_and(is_site, turn == 0)
    gives_near = jnp.logical_and(core == 0, turn == 0)

    @pl.when(uses_own)
    def _():
        own_morph.start()

    @pl.when(has_after)
    def _():
        pl.semaphore_wait(barrier, s0 + 1)

    @pl.when(s0 == n_space - 2)
    def _():
        pl.semaphore_signal(row_in, inc=1, device_id={"space": n_space - 1})

    @pl.when(last)
    def _():
        pl.semaphore_wait(row_in, 1)
        each(n_yaw, lambda d: pl.semaphore_signal(barrier, inc=1, device_id={"yaw": yaw_peer(d)}))
        pl.semaphore_wait(barrier, n_yaw)
        each(n_space - 1, lambda slab: pl.semaphore_signal(all_in, inc=1, device_id={"space": slab}), 0)

    def halo(slot, src, dst, peer):
        return pltpu.make_async_remote_copy(
            src_ref=src, dst_ref=dst, send_sem=halo_send.at[slot], recv_sem=halo_recv.at[slot],
            device_id={"space": peer},
        )

    up = (
        halo(0, adj.at[0, :, layers - 1], far_a.at[0], s0 + 1),
        halo(1, visc.at[0, layers - 1], far_v.at[0], s0 + 1),
    )
    down = (
        halo(2, adj_in.at[0, :, 0], far_a.at[1], s0 - 1),
        halo(3, visc_in.at[0, 0], far_v.at[1], s0 - 1),
    )

    @pl.when(jnp.logical_and(has_before, core == 0))
    def _():
        for copy in down:
            copy.start()

    for copy in loads[:2]:
        copy.wait()

    @pl.when(has_after)
    def _():
        for copy in up:
            copy.start()

    @pl.when(core == 1)
    def _():
        for copy in down:
            copy.start()

    for copy in loads[2:]:
        copy.start()

    @pl.when(gives_near)
    def _():
        near_morph.start()

    @pl.when(jnp.logical_not(has_before))
    def _():
        far_a[0] = jnp.zeros_like(far_a[0])
        far_v[0] = jnp.zeros_like(far_v[0])

    @pl.when(jnp.logical_not(has_after))
    def _():
        far_a[1] = jnp.zeros_like(far_a[1])
        far_v[1] = jnp.zeros_like(far_v[1])

    for copy in loads[2:]:
        copy.wait()

    at_y = lax.broadcasted_iota(jnp.int32, (ny, nz), 0)
    at_z = lax.broadcasted_iota(jnp.int32, (ny, nz), 1)
    shifts = (
        (0, 1, at_y > 0), (0, ny - 1, at_y < ny - 1), (1, 1, at_z > 0), (1, nz - 1, at_z < nz - 1)
    )
    for x in range(layers):
        v = visc[0, x]
        total = jnp.zeros_like(v)
        faces = []
        for axis, shift, inside in shifts:
            face = 0.5 * (v + jnp.where(inside, pltpu.roll(v, shift, axis), 0.0))
            total = total + face
            faces.append(jnp.where(inside, face, 0.0))
        inner = {}
        for nb in (x - 1, x + 1):
            if 0 <= nb < layers:
                inner[nb] = 0.5 * (v + visc[0, nb])
                total = total + inner[nb]
        total = total + 2.0
        acc = jnp.zeros_like(v)
        for f in range(fields):
            a = adj[0, f, x]
            out = total * a
            for g in range(fields):
                out = out + coup[0, f, g] * adj[0, g, x]
            for (axis, shift, _), face in zip(shifts, faces):
                out = out - face * pltpu.roll(a, shift, axis)
            for nb, face in inner.items():
                out = out - face * adj[0, f, nb]
            res[0, f, x] = out
            acc = acc + a * out
        inner_sens[x] = acc

    for j in range(nodes // CHUNK):
        at = pl.ds(j * CHUNK, CHUNK)
        low = patch[:, at] % LANES
        hot = (lax.broadcasted_iota(jnp.int32, (LANES, CHUNK), 0) == low).astype(F32)
        pick_patch_t[at, :] = hot.T.astype(BF16)
    normal8[...] = jnp.zeros_like(normal8)
    for h in range(halves):
        normal8[3 * h:3 * h + 3, :] = normal[...]

    @pl.when(uses_own)
    def _():
        own_morph.wait()

    @pl.when(gets_near)
    def _():
        near_morph.wait_recv()

    @pl.when(is_site)
    def _():
        m_hi, m_lo = parts(morph[...].T)
        morph_hi[...] = m_hi
        morph_lo[...] = m_lo

    def sens_of(side):
        x = side * (layers - 1)
        v = visc[0, x]
        across = jnp.zeros_like(v)
        for f in range(fields):
            a = adj[0, f, x]
            across = across + a * (far_a[side, f] - a)
        acc = inner_sens[x] - 0.5 * (v + far_v[side]) * across
        cell_sens[side] = weight[0] * v * acc

    def at_nodes(side, block):
        here = cell[8 * block:8 * block + 8]
        lane, row = here % LANES, here // LANES - side * ((layers - 1) * ny * groups)
        found = [jnp.zeros(lane.shape, F32)] * groups
        for y in range(ny):
            for g in range(groups):
                source = jnp.broadcast_to(cell_sens[side, y:y + 1, g * LANES:(g + 1) * LANES], lane.shape)
                value = jnp.take_along_axis(source, lane, axis=1, mode="promise_in_bounds")
                found[g] = jnp.where(row == y * groups + g, value, found[g])
        return sum(found[1:], found[0])

    @pl.when(jnp.logical_and(core == 0, has_after))
    def _():
        for copy in down:
            copy.wait_recv()

    @pl.when(core == 1)
    def _():
        for copy in up:
            copy.wait_recv()

    sens_of(1 - core)
    for block in range(nodes // (8 * LANES)):
        near_sens[8 * block:8 * block + 8] = at_nodes(1 - core, block)

    @pl.when(jnp.logical_and(core == 0, has_before))
    def _():
        for copy in up:
            copy.wait_recv()

    @pl.when(jnp.logical_and(core == 1, has_after))
    def _():
        for copy in down:
            copy.wait_recv()

    sens_of(core)
    owner_rows = n_space * rows
    wide = 8 * LANES
    shape3 = (n_space, rows, wide)
    half_of = lax.broadcasted_iota(jnp.int32, shape3, 0) * halves + lax.broadcasted_iota(jnp.int32, shape3, 1) // 3
    sums_now = jnp.zeros((2 * owner_rows, LANES), F32)
    for j in range(nodes // wide):
        at = pl.ds(j * wide, wide)
        sens = near_sens[8 * j:8 * j + 8] + at_nodes(core, j)
        part = jnp.concatenate([
            normal8[:, j * wide + r * LANES:j * wide + (r + 1) * LANES] * sens[r:r + 1] for r in range(8)
        ], axis=1)
        hi = part.astype(BF16).astype(F32)
        chosen = half_of == (patch[:, at] // LANES)[None]
        a = jnp.concatenate([
            jnp.where(chosen, piece[None], 0.0).reshape(owner_rows, wide).astype(BF16) for piece in (hi, part - hi)
        ], axis=0)
        sums_now = sums_now + dot(a, pick_patch_t[at, :])
    dense[...] = (sums_now[:owner_rows] + sums_now[owner_rows:]).reshape(dense.shape)

    pair = lax.div(y0, 2)

    def slot(yaw, slab):
        return lax.rem(y0 - yaw + n_yaw, n_yaw) * n_space + lax.rem(s0 - slab + n_space, n_space)

    def wait_blocks(sem, start, count):
        blocks = got.at[start:start + count, 0:used]
        pltpu.make_async_copy(blocks, blocks, sem).wait()

    def to_site(q, owner):
        odd = lax.rem(owner, 2)
        return pltpu.make_async_remote_copy(
            src_ref=dense.at[owner, 0:used],
            dst_ref=got.at[slot(2 * q + odd, owner - odd + 1), 0:used],
            send_sem=send1, recv_sem=recv1,
            device_id={"yaw": 2 * q + odd, "space": owner - odd + 1},
        )

    pl.when(has_after)(lambda: pl.semaphore_wait(all_in, 1))
    def to_sites(q, i):
        owner = n_space - 1 - i

        @pl.when(jnp.logical_not(jnp.logical_and(is_site, jnp.logical_and(pair == q, owner == mine))))
        def _():
            to_site(q, owner).start()

    for q in range(n_yaw // 2):
        each(n_space, functools.partial(to_sites, q), 0)

    for side in range(2):
        x = side * (layers - 1)
        face = 0.5 * (visc[0, x] + far_v[side])
        for f in range(fields):
            res[0, f, x] = res[0, f, x] - face * (far_a[side, f] - adj[0, f, x])

    def to_slab(k, slab):
        return pltpu.make_async_remote_copy(
            src_ref=grads.at[mine, 0:used], dst_ref=grads.at[mine, 0:used],
            send_sem=send3, recv_sem=recv3,
            device_id={"yaw": 2 * pair + k, "space": slab},
        )

    def to_slabs(slab):
        for k in range(2):
            @pl.when(jnp.logical_not(jnp.logical_and(slab == s0, turn == k)))
            def _():
                to_slab(k, slab).start()

    @pl.when(is_site)
    def _():
        got[0] = dense[mine]
        wait_blocks(recv1, 1, n_yaw * n_space - 1)
        p = jnp.sum(got[...], axis=0)
        p = jnp.concatenate([p[3 * h:3 * h + 3] for h in range(halves)], axis=1)
        p = jnp.concatenate([p, jnp.zeros((5, owned), F32)], axis=0)
        hi, lo = parts(p)
        both = jnp.concatenate([hi.astype(F32), lo.astype(F32)], axis=0).astype(BF16)
        smooth = dot(both, morph_hi[...]) + dot(both, morph_lo[...])
        g = p + smooth[0:8] + smooth[8:16]
        for h in range(halves):
            grads[mine, 3 * h:3 * h + 3] = g[0:3, h * LANES:(h + 1) * LANES]
        each(n_space, to_slabs, 0)

    @pl.when(has_before)
    def _():
        for copy in down:
            copy.wait_send()

    @pl.when(has_after)
    def _():
        for copy in up:
            copy.wait_send()

    @pl.when(gives_near)
    def _():
        near_morph.wait_send()

    sent = n_yaw // 2 * n_space

    @pl.when(is_site)
    def _():
        wait_blocks(send1, 0, sent - 1)
        wait_blocks(recv3, 0, n_space - 1)

    @pl.when(jnp.logical_not(is_site))
    def _():
        wait_blocks(send1, 0, sent)
        wait_blocks(recv3, 0, n_space)

    for h in range(halves):
        pgrad[:, h * LANES:(h + 1) * LANES] = grads[s0, 3 * h:3 * h + 3]
    grads_out[...] = grads[...]

    @pl.when(is_site)
    def _():
        wait_blocks(send3, 0, 2 * n_space - 1)


def finish(res, pgrad, grads, tile, res_out, pgrad_out, ngrad_out, ngrad, sem):
    n_space = grads.shape[0]
    halves = pgrad.shape[1] // LANES
    copies = [
        pltpu.make_async_copy(src, dst, sem.at[i])
        for i, (src, dst) in enumerate(((res, res_out), (pgrad, pgrad_out), (ngrad, ngrad_out)))
    ]
    for copy in copies[:2]:
        copy.start()
    for block in range(tile.shape[0] // 8):
        node_patch = tile[8 * block:8 * block + 8]
        low, high = node_patch % LANES, node_patch // LANES
        out = [jnp.zeros(low.shape, F32)] * 3
        for owner in range(n_space):
            for h in range(halves):
                here = high == owner * halves + h
                for c in range(3):
                    row = jnp.broadcast_to(grads[owner, 3 * h + c:3 * h + c + 1], low.shape)
                    value = jnp.take_along_axis(row, low, axis=1, mode="promise_in_bounds")
                    out[c] = jnp.where(here, value, out[c])
        for c in range(3):
            for r in range(8):
                at = (8 * block + r) * LANES
                ngrad[c:c + 1, at:at + LANES] = out[c][r:r + 1]
    copies[2].start()
    for copy in copies:
        copy.wait()


def shards(
    n_yaw, n_space,
    adjoint, viscosity, coupling, yaw_weight, node_cell, node_patch, node_normal, morph_kernel,
):
    _, fields, layers, ny, nz = adjoint.shape
    nodes = node_cell.shape[0]
    owned = morph_kernel.shape[1]
    rows = -(-3 * (owned // LANES) // 8) * 8
    vmem = pl.BlockSpec(memory_space=pltpu.VMEM)
    anywhere = pl.BlockSpec(memory_space=pl.ANY)
    dma = pltpu.SemaphoreType.DMA
    outs = pl.pallas_call(
        functools.partial(kernel, n_yaw, n_space),
        out_shape=(
            pltpu.VMEM(adjoint.shape, F32),
            pltpu.VMEM((3, owned), F32),
            pltpu.VMEM((n_space, rows, LANES), F32),
            pltpu.VMEM((nodes // LANES, LANES), jnp.int32),
        ),
        in_specs=[pl.BlockSpec(memory_space=pltpu.HBM)] * 9,
        out_specs=(vmem,) * 4,
        scratch_shapes=[
            pltpu.SMEM(coupling.shape, F32),
            pltpu.SMEM((1,), F32),
            pltpu.VMEM(adjoint.shape, F32),
            pltpu.VMEM(viscosity.shape, F32),
            pltpu.VMEM((nodes // LANES, LANES), jnp.int32),
            pltpu.VMEM((1, nodes), jnp.int32),
            pltpu.VMEM(node_normal.shape, F32),
            pltpu.VMEM(morph_kernel.shape, F32),
            pltpu.VMEM((2, fields, ny, nz), F32),
            pltpu.VMEM((2, ny, nz), F32),
            pltpu.VMEM((2, ny, nz), F32),
            pltpu.VMEM((nodes // LANES, LANES), F32),
            pltpu.VMEM((nodes, LANES), BF16),
            pltpu.VMEM((rows, nodes), F32),
            pltpu.VMEM((owned, owned), BF16),
            pltpu.VMEM((owned, owned), BF16),
            pltpu.VMEM((layers, ny, nz), F32),
            pltpu.VMEM((n_space, rows, LANES), F32),
            pltpu.VMEM((n_yaw * n_space, rows, LANES), F32),
            pltpu.VMEM((n_space, rows, LANES), F32),
            pltpu.SemaphoreType.REGULAR, pltpu.SemaphoreType.REGULAR,
            dma((9,)), dma((4,)), dma((4,)),
            dma, dma, dma, dma, dma, dma,
        ],
        compiler_params=pltpu.CompilerParams(
            collective_id=0, has_side_effects=True, vmem_limit_bytes=56 * 1024 * 1024
        ),
        cost_estimate=pl.CostEstimate(flops=400_000_000, bytes_accessed=1_000_000, transcendentals=0),
    )(
        coupling, yaw_weight, adjoint, viscosity,
        node_cell.reshape(nodes // LANES, LANES), node_patch[None], node_patch.reshape(nodes // LANES, LANES), node_normal, morph_kernel,
    )
    return pl.pallas_call(
        finish,
        out_shape=(
            jax.ShapeDtypeStruct(adjoint.shape, F32),
            jax.ShapeDtypeStruct((3, owned), F32),
            jax.ShapeDtypeStruct((3, nodes), F32),
        ),
        in_specs=[vmem] * 4,
        out_specs=(anywhere,) * 3,
        scratch_shapes=[pltpu.VMEM((3, nodes), F32), dma((3,))],
        compiler_params=pltpu.CompilerParams(vmem_limit_bytes=4 * 1024 * 1024),
    )(*outs)


def solution(mesh):
    return jax.shard_map(
        functools.partial(shards, mesh.shape["yaw"], mesh.shape["space"]),
        mesh=mesh,
        in_specs=(
            P("yaw", None, "space", None, None),
            P("yaw", "space", None, None),
            P("yaw", None, None),
            P("yaw"),
            P("space"),
            P("space"),
            P(None, "space"),
            P("space", None),
        ),
        out_specs=(P("yaw", None, "space", None, None), P(None, "space"), P(None, "space")),
        check_vma=False,
    )
```
